32 devices in a mesh: groups: 2 (over y), wid: 8 (over z, x), hgt: 1, tp: 2 (over core).
Axes of the slice: x: 2, y: 2, z: 4, core: 2. Of those that a mesh axis runs over, the one named last changes fastest.
Arguments:
- self_query: bfloat16 [4, 8, 64, 2560], P('groups', 'hgt', 'wid', 'tp'), parts along dimension 0, may hold values from -250 to 250
- self_key: bfloat16 [4, 8, 64, 2560], P('groups', 'hgt', 'wid', 'tp'), parts along dimension 0, may hold values from -250 to 250
- self_value: bfloat16 [4, 8, 64, 2560], P('groups', 'hgt', 'wid', 'tp'), parts along dimension 0, may hold values from -6 to 6
- cross_query: bfloat16 [4, 8, 64, 2560], P('groups', 'hgt', 'wid', 'tp'), parts along dimension 0, may hold values from -250 to 250
- text_key: bfloat16 [1024, 2560], P(('groups', 'wid'), 'tp'), parts along dimension 0, may hold values from -25 to 25
- text_value: bfloat16 [1024, 2560], P(('groups', 'wid'), 'tp'), parts along dimension 0, may hold values from -6 to 6
- image_key: bfloat16 [514, 2560], P('groups', 'tp'), parts along dimension 0, may hold values from -25 to 25
- image_value: bfloat16 [514, 2560], P('groups', 'tp'), parts along dimension 0, may hold values from -6 to 6
- query_gain: float32 [2560], P('tp'), may hold values from 0.1 to 1.9
- key_gain: float32 [2560], P('tp'), may hold values from 0.1 to 1.9
- cross_gain: float32 [2560], P('tp'), may hold values from 0.1 to 1.9
- windows: int32 [20, 3], P('tp'), may hold values from 0 to 2, as said below
Outputs:
- self_out: bfloat16 [4, 8, 64, 2560], P('groups', 'hgt', 'wid', 'tp'), parts along dimension 0
- cross_out: bfloat16 [4, 8, 64, 2560], P('groups', 'hgt', 'wid', 'tp'), parts along dimension 0
The draws below stay inside these ranges and needn't reach their ends.
There are 2 independent parts, one for each index of `groups`. The reference program is written for one: setup_inputs(seed, part) draws one part's arguments, and reference() takes and returns one part's arrays. A program takes and returns all parts, laid end to end along the dimension named above; an argument that names none is the same for every part. Nothing has to cross between parts.
Inputs may be any that keep to these rules, and one draw needn't show every extreme that they name: windows[n] holds head n's reach in frames, in height tiles and in width tiles; the last two are 0 or 1; some head has the reach (2, 1, 1).
All inputs are finite; a program needn't handle non-finite values.
Results may differ from the reference program's by a relative error of at most 0.0081.
Values may be sent and summed in bfloat16 or wider, within the bound.
A program may use at most 64 MiB of HBM per device.

```python
import math
import jax
import jax.numpy as jnp
from jax import lax

FRAMES = 2
ROWS_DEV = 8
COLS_DEV = 8
TILE = 4
FRAME_REACH = 2
HEADS = 20
HEAD_DIM = 128
TEXT_LEN = 512
IMAGE_LEN = 257
CHANNELS = 2560
HEIGHT = 8
WIDTH = 64
N_WID = 8
N_HGT = 1


def token_field(key, salt):
    base_key = jax.random.fold_in(key, salt)
    noise_key, row_key, col_key = jax.random.split(base_key, 3)
    position = jnp.arange(CHANNELS, dtype=jnp.float32) / CHANNELS
    noise = jnp.clip(jax.random.normal(noise_key, (FRAMES, HEIGHT, WIDTH, CHANNELS), jnp.float32), -4.0, 4.0)
    rising = jnp.exp(position * math.log(3.0))
    row_scale = jnp.exp(jax.random.uniform(row_key, (FRAMES, HEIGHT, WIDTH, 1), jnp.float32, 0.0, math.log(10.0)))
    rough = jnp.exp(jax.random.uniform(col_key, (CHANNELS,), jnp.float32, math.log(0.7), math.log(1.4)))
    return noise * row_scale * rising * rough


def draw_self_query(key, part):
    tokens = token_field(key, 11)
    return tokens.astype(jnp.bfloat16)


def draw_self_key(key, part):
    tokens = token_field(key, 12)
    return tokens.astype(jnp.bfloat16)


def draw_cross_query(key, part):
    tokens = token_field(key, 13)
    return tokens.astype(jnp.bfloat16)


def context_keys(key, salt, length):
    base_key = jax.random.fold_in(key, salt)
    rows_all = 2.5 * jnp.clip(jax.random.normal(base_key, (length, CHANNELS), jnp.float32), -4.0, 4.0)
    return rows_all


def draw_text_key(key, part):
    return context_keys(key, 14, TEXT_LEN).astype(jnp.bfloat16)


def draw_image_key(key, part):
    return context_keys(key, 15, IMAGE_LEN).astype(jnp.bfloat16)


def draw_windows(key, part):
    win_keys = jax.random.split(jax.random.fold_in(key, 21), 4)
    frame_win = jax.random.randint(win_keys[0], (HEADS,), 0, FRAME_REACH + 1)
    row_win = jax.random.randint(win_keys[1], (HEADS,), 0, 2)
    col_win = jax.random.randint(win_keys[2], (HEADS,), 0, 2)
    widest = jax.random.randint(win_keys[3], (), 0, HEADS)
    chosen = jnp.arange(HEADS, dtype=jnp.int32) == widest
    frame_win = jnp.where(chosen, FRAME_REACH, frame_win)
    row_win = jnp.where(chosen, 1, row_win)
    col_win = jnp.where(chosen, 1, col_win)
    return jnp.stack((frame_win, row_win, col_win), axis=1).astype(jnp.int32)


def block_scale(rng, extent, shards, smallest, largest):
    level, own = 1.0, jax.random.fold_in(rng, 6)
    for axis_at, blocks in shards:
        heights = jnp.exp(jax.random.uniform(jax.random.fold_in(own, axis_at), (blocks,), jnp.float32, smallest / len(shards), largest / len(shards)))
        level = level * jnp.repeat(heights, extent[axis_at] // blocks).reshape([-1 if axis == axis_at else 1 for axis in range(len(extent))])
    return level


def normal_values(stream_key, shape, width, limit, cuts=(), kind=jnp.bfloat16):
    array = jax.random.normal(stream_key, shape, jnp.float32) * width
    if len(cuts) > 0:
        array = block_scale(stream_key, shape, cuts, -0.22, 0.18) * array
    return jnp.clip(array, min=-limit, max=limit).astype(kind)


def setup_inputs(seed: int = 0, part: int = 0) -> dict:
    streams_of = jax.random.split(jax.random.key(seed), 13)
    part_keys = jax.random.split(jax.random.fold_in(streams_of[12], part), 13)
    self_query = draw_self_query(jax.random.fold_in(jax.random.fold_in(streams_of[12], part), 71), part)
    self_key = draw_self_key(jax.random.fold_in(jax.random.fold_in(streams_of[12], part), 71), part)
    self_value = normal_values(part_keys[2], (FRAMES, HEIGHT, WIDTH, CHANNELS), 1.0, 6.0, ((2, 8), (3, 2)))
    cross_query = draw_cross_query(jax.random.fold_in(jax.random.fold_in(streams_of[12], part), 71), part)
    text_key = draw_text_key(jax.random.fold_in(jax.random.fold_in(streams_of[12], part), 71), part)
    text_value = normal_values(part_keys[5], (TEXT_LEN, CHANNELS), 1.0, 6.0, ((0, 8), (1, 2)))
    image_key = draw_image_key(jax.random.fold_in(jax.random.fold_in(streams_of[12], part), 71), part)
    image_value = normal_values(part_keys[7], (IMAGE_LEN, CHANNELS), 1.0, 6.0, ((1, 2),))
    query_gain = jnp.clip(1.0 + 0.18 * jax.random.normal(streams_of[8], (CHANNELS,), jnp.float32), 0.1, 1.9)
    key_gain = jnp.clip(1.0 + 0.18 * jax.random.normal(streams_of[9], (CHANNELS,), jnp.float32), 0.1, 1.9)
    cross_gain = jnp.clip(1.0 + 0.18 * jax.random.normal(streams_of[10], (CHANNELS,), jnp.float32), 0.1, 1.9)
    windows = draw_windows(jax.random.fold_in(streams_of[12], 71), part)
    return {"self_query": self_query, "self_key": self_key, "self_value": self_value, "cross_query": cross_query, "text_key": text_key, "text_value": text_value, "image_key": image_key, "image_value": image_value, "query_gain": query_gain, "key_gain": key_gain, "cross_gain": cross_gain, "windows": windows}


epsilon = 1e-06
masked = -1e+30

def normalize(field, gain):
    wide = field.astype(jnp.float32)
    inverse = lax.rsqrt(lax.optimization_barrier(jnp.mean(wide * wide, axis=-1, keepdims=True)) + epsilon)
    return (wide * inverse * gain).astype(jnp.bfloat16)

def grid_positions(frame_count, row_count, col_count, row_start, col_start):
    full_shape = (frame_count, row_count, col_count)
    frame_ids = jnp.arange(frame_count, dtype=jnp.int32)[:, None, None]
    row_ids = jnp.arange(row_count, dtype=jnp.int32)[None, :, None] + row_start
    col_ids = jnp.arange(col_count, dtype=jnp.int32)[None, None, :] + col_start
    return (jnp.broadcast_to(frame_ids, full_shape).reshape(-1), jnp.broadcast_to(row_ids, full_shape).reshape(-1), jnp.broadcast_to(col_ids, full_shape).reshape(-1))

def window_mask(windows, query_pos, key_pos):
    inside = (key_pos[1] >= 0) & (key_pos[1] < HEIGHT) & (key_pos[2] >= 0) & (key_pos[2] < WIDTH)
    frame_gap = jnp.abs(query_pos[0][:, None] - key_pos[0][None, :])
    row_gap = jnp.abs(query_pos[1][:, None] // TILE - key_pos[1][None, :] // TILE)
    col_gap = jnp.abs(query_pos[2][:, None] // TILE - key_pos[2][None, :] // TILE)
    return (frame_gap[None] <= windows[:, 0, None, None]) & (row_gap[None] <= windows[:, 1, None, None]) & (col_gap[None] <= windows[:, 2, None, None]) & inside[None, None, :]

def attend(queries, key_rows, value_rows, allowed):
    factor = 1.0 / math.sqrt(HEAD_DIM)
    scores = jnp.einsum('qhd,khd->hqk', queries.astype(jnp.float32), key_rows.astype(jnp.float32)) * factor
    if allowed is not None:
        scores = jnp.where(allowed, scores, masked)
    row_top = lax.optimization_barrier(jnp.max(scores, axis=-1, keepdims=True))
    powers = jnp.exp(scores - row_top)
    if allowed is not None:
        powers = jnp.where(allowed, powers, 0.0)
    weights = lax.optimization_barrier(powers.astype(jnp.bfloat16)).astype(jnp.float32)
    numerator = jnp.einsum('hqk,khd->hqd', weights, value_rows.astype(jnp.float32))
    return numerator / lax.optimization_barrier(jnp.sum(powers, axis=-1))[..., None]

def unblock(blocks):
    shaped = blocks.reshape(N_HGT, N_WID, HEADS, FRAMES, ROWS_DEV, COLS_DEV, HEAD_DIM)
    return jnp.transpose(shaped, (3, 0, 4, 1, 5, 2, 6)).reshape(FRAMES, HEIGHT, WIDTH, CHANNELS)

def reference(self_query, self_key, self_value, cross_query, text_key, text_value, image_key, image_value, query_gain, key_gain, cross_gain, windows):
    q_normed = normalize(self_query, query_gain)
    k_normed = normalize(self_key, key_gain)
    x_normed = normalize(cross_query, cross_gain)
    margin = ((0, 0), (TILE, TILE), (TILE, TILE), (0, 0))
    k_padded = jnp.pad(k_normed, margin)
    v_padded = jnp.pad(self_value, margin)
    text_keys = text_key.reshape(TEXT_LEN, HEADS, HEAD_DIM)
    text_values = text_value.reshape(TEXT_LEN, HEADS, HEAD_DIM)
    image_keys = image_key.reshape(IMAGE_LEN, HEADS, HEAD_DIM)
    image_values = image_value.reshape(IMAGE_LEN, HEADS, HEAD_DIM)
    zero_index = jnp.zeros((), jnp.int32)
    inner_size = (FRAMES, ROWS_DEV, COLS_DEV, CHANNELS)
    outer_size = (FRAMES, ROWS_DEV + 2 * TILE, COLS_DEV + 2 * TILE, CHANNELS)

    def one_block(block_index):
        row_start = (block_index // N_WID * ROWS_DEV).astype(jnp.int32)
        col_start = (block_index % N_WID * COLS_DEV).astype(jnp.int32)
        corner = (zero_index, row_start, col_start, zero_index)
        queries = lax.dynamic_slice(q_normed, corner, inner_size).reshape(-1, HEADS, HEAD_DIM)
        crosses = lax.dynamic_slice(x_normed, corner, inner_size).reshape(-1, HEADS, HEAD_DIM)
        key_rows = lax.dynamic_slice(k_padded, corner, outer_size).reshape(-1, HEADS, HEAD_DIM)
        value_rows = lax.dynamic_slice(v_padded, corner, outer_size).reshape(-1, HEADS, HEAD_DIM)
        query_pos = grid_positions(FRAMES, ROWS_DEV, COLS_DEV, row_start, col_start)
        key_pos = grid_positions(FRAMES, ROWS_DEV + 2 * TILE, COLS_DEV + 2 * TILE, row_start - TILE, col_start - TILE)
        allowed = window_mask(windows, query_pos, key_pos)
        self_heads = attend(queries, key_rows, value_rows, allowed)
        cross_heads = attend(crosses, text_keys, text_values, None) + attend(crosses, image_keys, image_values, None)
        return (self_heads.astype(jnp.bfloat16), cross_heads.astype(jnp.bfloat16))
    self_blocks, cross_blocks = lax.map(one_block, jnp.arange(N_HGT * N_WID, dtype=jnp.int32))
    return (unblock(self_blocks), unblock(cross_blocks))
```

```python
import functools
import math

import jax
import jax.numpy as jnp
from jax import lax
from jax.experimental import pallas as pl
from jax.experimental.pallas import tpu as pltpu
from jax.sharding import PartitionSpec as P

TILE = 4


epsilon = 1e-06
masked = -1e30


def padded(value, sides, width):
    for axis, dim in sides:
        count, length = (lax.axis_size(axis), value.shape[dim])
        up = [(i, (i + 1) % count) for i in range(count - 1)]
        down = [(j, i) for i, j in up]
        last = lax.slice_in_dim(value, length - width, length, axis=dim)
        first = lax.slice_in_dim(value, 0, width, axis=dim)
        before = lax.ppermute(last, axis, up)
        after = lax.ppermute(first, axis, down)
        value = jnp.concatenate([before, value, after], axis=dim)
    return value


def grid_positions(frame_count, row_count, col_count, row_start, col_start):
    full_shape = (frame_count, row_count, col_count)
    frame_ids = jnp.arange(frame_count, dtype=jnp.int32)[:, None, None]
    row_ids = jnp.arange(row_count, dtype=jnp.int32)[None, :, None] + row_start
    col_ids = jnp.arange(col_count, dtype=jnp.int32)[None, None, :] + col_start
    return (
        jnp.broadcast_to(frame_ids, full_shape).reshape(-1),
        jnp.broadcast_to(row_ids, full_shape).reshape(-1),
        jnp.broadcast_to(col_ids, full_shape).reshape(-1),
    )


def window_mask(windows, query_pos, key_pos, height_all, width_all):
    inside = (
        (key_pos[1] >= 0) & (key_pos[1] < height_all) & (key_pos[2] >= 0) & (key_pos[2] < width_all)
    )
    frame_gap = jnp.abs(query_pos[0][:, None] - key_pos[0][None, :])
    row_gap = jnp.abs(query_pos[1][:, None] // TILE - key_pos[1][None, :] // TILE)
    col_gap = jnp.abs(query_pos[2][:, None] // TILE - key_pos[2][None, :] // TILE)
    return (
        (frame_gap[None] <= windows[:, 0, None, None])
        & (row_gap[None] <= windows[:, 1, None, None])
        & (col_gap[None] <= windows[:, 2, None, None])
        & inside[None, None, :]
    )


def attend_part(queries, key_rows, value_rows, allowed):
    factor = 1.0 / math.sqrt(queries.shape[-1])
    scores = (
        jnp.einsum("qhd,khd->hqk", queries, key_rows, preferred_element_type=jnp.float32) * factor
    )
    if allowed is not None:
        scores = jnp.where(allowed, scores, masked)
    row_top = jnp.max(scores, axis=-1)
    powers = jnp.exp(scores - row_top[..., None])
    if allowed is not None:
        powers = jnp.where(allowed, powers, 0.0)
    weights = powers.astype(jnp.bfloat16)
    numerator = jnp.einsum("hqk,khd->hqd", weights, value_rows, preferred_element_type=jnp.float32)
    return (row_top, jnp.sum(powers, axis=-1), numerator)


def merge_parts(first, second):
    row_top = jnp.maximum(first[0], second[0])
    upper = jnp.exp(second[0] - row_top)
    return (row_top, second[1] * upper, second[2] * upper[..., None])


def finish_part(part, frame_count, row_count, col_count):
    heads_out = part[2] / part[1][..., None]
    return jnp.transpose(heads_out, (1, 0, 2)).reshape(frame_count, row_count, col_count, -1)


def sum_squares(field):
    wide = field.astype(jnp.float32)
    return jnp.sum(wide * wide, axis=-1)


def apply_norm(field, squares_all, channel_total, gain):
    inverse = lax.rsqrt(squares_all / channel_total + epsilon)
    return (field.astype(jnp.float32) * inverse[..., None] * gain).astype(jnp.bfloat16)


def flat_heads(field, head_count):
    return field.reshape(-1, head_count, field.shape[-1] // head_count)


def body(
    self_query,
    self_key,
    self_value,
    cross_query,
    text_key,
    text_value,
    image_key,
    image_value,
    query_gain,
    key_gain,
    cross_gain,
    windows,
):
    frame_count, row_count, col_count, channels = self_query.shape
    head_count = windows.shape[0]
    channel_total = channels * lax.axis_size("tp")
    height_all = row_count * lax.axis_size("hgt")
    width_all = col_count * lax.axis_size("wid")
    row_start = lax.axis_index("hgt") * row_count
    col_start = lax.axis_index("wid") * col_count
    squares_all = lax.psum(
        (sum_squares(self_query), sum_squares(self_key), sum_squares(cross_query)), "tp"
    )
    q_normed = apply_norm(self_query, squares_all[0], channel_total, query_gain)
    k_normed = apply_norm(self_key, squares_all[1], channel_total, key_gain)
    x_normed = apply_norm(cross_query, squares_all[2], channel_total, cross_gain)
    queries = flat_heads(q_normed, head_count)
    query_pos = grid_positions(frame_count, row_count, col_count, row_start, col_start)
    stacked = jnp.stack((k_normed, self_value))
    extended = padded(stacked, (("wid", 3), ("hgt", 2)), TILE)
    key_pos = grid_positions(
        frame_count, row_count + 2 * TILE, col_count + 2 * TILE, row_start - TILE, col_start - TILE
    )
    allowed = window_mask(windows, query_pos, key_pos, height_all, width_all)
    self_part = attend_part(
        queries, flat_heads(extended[0], head_count), flat_heads(extended[1], head_count), allowed
    )
    self_out = finish_part(self_part, frame_count, row_count, col_count).astype(jnp.bfloat16)
    crosses = flat_heads(x_normed, head_count)
    query_total = crosses.shape[0]
    start_part = (
        jnp.full((head_count, query_total), masked, jnp.float32),
        jnp.zeros((head_count, query_total), jnp.float32),
        jnp.zeros((head_count, query_total, crosses.shape[-1]), jnp.float32),
    )
    fresh = attend_part(
        crosses,
        flat_heads(lax.all_gather(text_key, "wid", axis=0, tiled=True), head_count),
        flat_heads(lax.all_gather(text_value, "wid", axis=0, tiled=True), head_count),
        None,
    )
    text_part = merge_parts(start_part, fresh)
    image_part = attend_part(
        crosses, flat_heads(image_key, head_count), flat_heads(image_value, head_count), None
    )
    cross_out = (
        finish_part(text_part, frame_count, row_count, col_count)
        + finish_part(image_part, frame_count, row_count, col_count)
    ).astype(jnp.bfloat16)
    return (self_out, cross_out)


MESH = pl.DeviceIdType.MESH


def squares_of(ref, head_count, depth, tokens):
    total = jnp.zeros((tokens, depth), jnp.float32)
    for head in range(head_count):
        wide = head_block(ref, head * depth, depth, tokens)
        total = total + wide * wide
    return jnp.sum(total, axis=-1, keepdims=True)


def head_block(ref, start, depth, tokens):
    block = ref[:, :, :, pl.ds(start, depth)]
    return block.astype(jnp.float32).reshape(tokens, depth)


def dot_nt(left, right):
    return lax.dot_general(
        left, right, (((1,), (1,)), ((), ())), preferred_element_type=jnp.float32
    )


def soft_mix(scores, value_rows, factor):
    row_top = jnp.max(scores, axis=-1, keepdims=True)
    powers = jnp.exp((scores - row_top) * factor)
    total = jnp.sum(powers, axis=-1, keepdims=True)
    mixed = jnp.dot(
        powers.astype(jnp.bfloat16), value_rows, preferred_element_type=jnp.float32
    )
    return mixed * (1.0 / total)


def fused(
    wid_count,
    head_count,
    sq_ref,
    sk_ref,
    sv_ref,
    xq_ref,
    tk_ref,
    tv_ref,
    ik_ref,
    iv_ref,
    qg_ref,
    kg_ref,
    xg_ref,
    win_ref,
    so_ref,
    co_ref,
    text,
    text_out,
    keys,
    values,
    stat,
    stat_in,
    cross,
    cross_send,
    image_part,
    back_send,
    back_in,
    gaps,
    text_recv,
    up_send,
    down_send,
    side_send,
    halo_send,
    halo_recv,
    stat_send,
    stat_recv,
    cross_sem,
    back_send_sem,
    back_recv_sem,
):
    frames, rows, cols, channels = sq_ref.shape
    tokens = frames * rows * cols
    depth = channels // head_count
    half_heads = head_count // 2
    half = half_heads * depth
    edge = frames * rows * TILE
    col_tiles = cols // TILE
    lines = wid_count // 2
    factor = 1.0 / math.sqrt(depth)

    w = lax.axis_index("wid")
    core = lax.axis_index("tp")
    line = w // 2
    side = w % 2
    mate = line * 2 + (1 - side)
    not_first, not_last = w > 0, w < wid_count - 1
    has_down, has_up = line > 0, line < lines - 1

    def at_wid(target):
        return {"wid": target}

    barrier = pltpu.get_barrier_semaphore()
    pl.semaphore_signal(barrier, inc=1, device_id={"tp": 1 - core}, device_id_type=MESH)
    for cond, target in (
        (not_first, w - 1),
        (not_last, w + 1),
        (has_down, w - 2),
        (has_up, w + 2),
    ):

        @pl.when(cond)
        def _():
            pl.semaphore_signal(barrier, inc=1, device_id=at_wid(target), device_id_type=MESH)

    mine = pl.multiple_of(side * half, depth)
    other = pl.multiple_of((1 - side) * half, depth)
    text[w, 0] = tk_ref[:, pl.ds(mine, half)]
    text[w, 1] = tv_ref[:, pl.ds(mine, half)]
    text_out[0] = tk_ref[:, pl.ds(other, half)]
    text_out[1] = tv_ref[:, pl.ds(other, half)]
    expected = 1
    for cond in (not_first, not_last, has_down, has_up):
        expected = expected + jnp.where(cond, 1, 0)
    pl.semaphore_wait(barrier, expected)

    def relay(slot, up):
        return pltpu.make_async_remote_copy(
            src_ref=text.at[slot],
            dst_ref=text.at[slot],
            send_sem=(up_send if up else down_send).at[slot],
            recv_sem=text_recv.at[slot],
            device_id=at_wid(w + 2 if up else w - 2),
            device_id_type=MESH,
        )

    def forward(slot, up):
        @pl.when(has_up if up else has_down)
        def _():
            relay(slot, up).start()

    def take(slot):
        pltpu.make_async_remote_copy(
            src_ref=text.at[slot],
            dst_ref=text.at[slot],
            send_sem=side_send,
            recv_sem=text_recv.at[slot],
            device_id=at_wid(mate),
            device_id_type=MESH,
        ).wait_recv()

    def relay_step(step, which):
        below, above = (line - step) * 2 + which, (line + step) * 2 + which

        @pl.when(line - step >= 0)
        def _():
            take(below)
            forward(below, True)

        @pl.when(line + step < lines)
        def _():
            take(above)
            forward(above, False)

    forward(w, True)
    forward(w, False)
    side_copy = pltpu.make_async_remote_copy(
        src_ref=text_out,
        dst_ref=text.at[w],
        send_sem=side_send,
        recv_sem=text_recv.at[w],
        device_id=at_wid(mate),
        device_id_type=MESH,
    )
    side_copy.start()

    lane = lax.broadcasted_iota(jnp.int32, (tokens, depth), 1)
    sums = [squares_of(ref, head_count, depth, tokens) for ref in (sq_ref, sk_ref, xq_ref)]
    stat[...] = jnp.where(lane == 0, sums[0], jnp.where(lane == 1, sums[1], sums[2]))
    stat_copy = pltpu.make_async_remote_copy(
        src_ref=stat,
        dst_ref=stat_in,
        send_sem=stat_send,
        recv_sem=stat_recv,
        device_id={"tp": 1 - core},
        device_id_type=MESH,
    )
    stat_copy.start()

    place = lax.broadcasted_iota(jnp.int32, (tokens, tokens), 0)
    source = lax.broadcasted_iota(jnp.int32, (tokens, tokens), 1)
    inner = lax.rem(place, edge)
    natural = (
        lax.div(inner, rows * TILE) * (rows * cols)
        + lax.rem(lax.div(inner, TILE), rows) * cols
        + lax.div(place, edge) * TILE
        + lax.rem(inner, TILE)
    )
    to_tiles = jnp.where(natural == source, 1.0, 0.0).astype(jnp.bfloat16)

    def tile_order(block):
        return jnp.dot(to_tiles, block, preferred_element_type=jnp.float32).astype(jnp.bfloat16)

    def halo(ref, at, down):
        return pltpu.make_async_remote_copy(
            src_ref=ref.at[pl.ds(edge if down else tokens, edge)],
            dst_ref=ref.at[pl.ds(edge + tokens if down else 0, edge)],
            send_sem=halo_send.at[at],
            recv_sem=halo_recv.at[at],
            device_id=at_wid(w - 1 if down else w + 1),
            device_id_type=MESH,
        )

    def start_halo(ref, at):
        @pl.when(not_first)
        def _():
            halo(ref, at, True).start()

        @pl.when(not_last)
        def _():
            halo(ref, at + 1, False).start()

    @pl.when(w == 0)
    def _():
        for ref in (keys, values):
            ref[0:edge] = jnp.zeros((edge, channels), jnp.bfloat16)

    @pl.when(w == wid_count - 1)
    def _():
        for ref in (keys, values):
            ref[edge + tokens :] = jnp.zeros((edge, channels), jnp.bfloat16)

    for head in range(head_count):
        block = head_block(sv_ref, head * depth, depth, tokens).astype(jnp.bfloat16)
        values[edge : edge + tokens, head * depth : (head + 1) * depth] = tile_order(block)
    start_halo(values, 2)

    stat_copy.wait()
    whole = stat[...] + stat_in[...]
    inverse = lax.rsqrt(whole / (channels * 2) + epsilon)
    inverse_q, inverse_k, inverse_x = inverse[:, 0:1], inverse[:, 1:2], inverse[:, 2:3]

    def normed(ref, gain_ref, start, inverse_of):
        wide = head_block(ref, start, depth, tokens)
        return (wide * inverse_of * gain_ref[:, pl.ds(start, depth)]).astype(jnp.bfloat16)

    for head in range(head_count):
        block = normed(sk_ref, kg_ref, head * depth, inverse_k)
        keys[edge : edge + tokens, head * depth : (head + 1) * depth] = tile_order(block)
    start_halo(keys, 0)

    for head in range(half_heads):
        at = pl.multiple_of((1 - side) * half + head * depth, depth)
        cross_send[:, head * depth : (head + 1) * depth] = normed(xq_ref, xg_ref, at, inverse_x)
    cross_copy = pltpu.make_async_remote_copy(
        src_ref=cross_send,
        dst_ref=cross.at[pl.ds(tokens, tokens)],
        send_sem=cross_sem.at[0],
        recv_sem=cross_sem.at[1],
        device_id=at_wid(mate),
        device_id_type=MESH,
    )
    cross_copy.start()

    take(mate)
    forward(mate, True)
    forward(mate, False)

    for head in range(half_heads):
        at = pl.multiple_of(side * half + head * depth, depth)
        cross[0:tokens, head * depth : (head + 1) * depth] = normed(xq_ref, xg_ref, at, inverse_x)

    spread = (tokens, tokens + 2 * edge)
    query = lax.broadcasted_iota(jnp.int32, spread, 0)
    key = lax.broadcasted_iota(jnp.int32, spread, 1)
    key_tile = lax.div(key, edge) - 1
    key_inner = lax.rem(key, edge)
    key_col = key_tile + w * col_tiles
    inside = (key_col >= 0) & (key_col < wid_count * col_tiles)
    frame_gap = jnp.abs(lax.div(query, rows * cols) - lax.div(key_inner, rows * TILE))
    row_gap = jnp.abs(
        lax.div(lax.rem(lax.div(query, cols), rows), TILE)
        - lax.div(lax.rem(lax.div(key_inner, TILE), rows), TILE)
    )
    col_gap = jnp.abs(lax.div(lax.rem(query, cols), TILE) - key_tile)
    gaps[0] = jnp.where(inside, frame_gap, 1 << 30)
    gaps[1] = row_gap
    gaps[2] = col_gap

    def self_head(head):
        at = slice(head * depth, (head + 1) * depth)
        queries = normed(sq_ref, qg_ref, head * depth, inverse_q)
        scores = dot_nt(queries, keys[:, at])
        allowed = (
            (gaps[0] <= win_ref[head, 0])
            & (gaps[1] <= win_ref[head, 1])
            & (gaps[2] <= win_ref[head, 2])
        )
        mixed = soft_mix(jnp.where(allowed, scores, masked), values[:, at], factor)
        so_ref[:, :, :, at] = mixed.reshape(frames, rows, cols, depth).astype(jnp.bfloat16)

    def image_head(head):
        at = slice(head * depth, (head + 1) * depth)
        there = pl.ds(pl.multiple_of(side * half + head * depth, depth), depth)
        scores = dot_nt(cross[:, at], ik_ref[:, there])
        image_part[:, at] = soft_mix(scores, iv_ref[:, there], factor)

    cross_copy.wait_recv()
    steps = [(step, turn) for step in range(1, lines) for turn in range(2)]

    def next_step():
        if steps:
            step, turn = steps.pop(0)
            relay_step(step, side if turn == 0 else 1 - side)

    next_step()
    for head in range(half_heads):
        image_head(head)
        if head == half_heads // 2:
            next_step()
    next_step()

    def wait_halo(ref, at):
        @pl.when(not_last)
        def _():
            halo(ref, at, True).wait_recv()

        @pl.when(not_first)
        def _():
            halo(ref, at + 1, False).wait_recv()

    wait_halo(values, 2)
    wait_halo(keys, 0)
    for head in range(head_count):
        self_head(head)
        if head == head_count // 2 - 1:
            next_step()
    while steps:
        next_step()

    backs = []
    for head in range(half_heads):
        at = slice(head * depth, (head + 1) * depth)
        rows_all = wid_count * tk_ref.shape[0]
        scores = dot_nt(cross[:, at], text[:, 0, :, at].reshape(rows_all, depth))
        mixed = soft_mix(scores, text[:, 1, :, at].reshape(rows_all, depth), factor)
        mixed = mixed + image_part[:, at]
        back_send[head] = mixed[tokens:].astype(jnp.bfloat16)
        back = pltpu.make_async_remote_copy(
            src_ref=back_send.at[head],
            dst_ref=back_in.at[head],
            send_sem=back_send_sem.at[head],
            recv_sem=back_recv_sem.at[head],
            device_id=at_wid(mate),
            device_id_type=MESH,
        )
        back.start()
        backs.append(back)
        there = pl.ds(pl.multiple_of(side * half + head * depth, depth), depth)
        own = mixed[:tokens].reshape(frames, rows, cols, depth)
        co_ref[:, :, :, there] = own.astype(jnp.bfloat16)

    side_copy.wait_send()
    cross_copy.wait_send()
    for at, ref in ((0, keys), (2, values)):

        @pl.when(not_first)
        def _():
            halo(ref, at, True).wait_send()

        @pl.when(not_last)
        def _():
            halo(ref, at + 1, False).wait_send()

    for place_line in range(lines):
        for place_side in range(2):
            slot = place_line * 2 + place_side

            @pl.when(has_up & (place_line <= line))
            def _():
                relay(slot, True).wait_send()

            @pl.when(has_down & (place_line >= line))
            def _():
                relay(slot, False).wait_send()

    for head in range(half_heads):
        backs[head].wait()
        there = pl.ds(pl.multiple_of((1 - side) * half + head * depth, depth), depth)
        came = back_in[head].astype(jnp.float32).reshape(frames, rows, cols, depth)
        co_ref[:, :, :, there] = came.astype(jnp.bfloat16)


def fused_body(
    wid_count,
    self_query,
    self_key,
    self_value,
    cross_query,
    text_key,
    text_value,
    image_key,
    image_value,
    query_gain,
    key_gain,
    cross_gain,
    windows,
):
    frames, rows, cols, channels = self_query.shape
    tokens = frames * rows * cols
    head_count = windows.shape[0]
    depth = channels // head_count
    half_heads = head_count // 2
    half = half_heads * depth
    edge = frames * rows * TILE
    text_rows = text_key.shape[0]
    bf16, f32 = jnp.bfloat16, jnp.float32
    dma = pltpu.SemaphoreType.DMA
    vmem = pl.BlockSpec(memory_space=pltpu.VMEM)
    return pl.pallas_call(
        functools.partial(fused, wid_count, head_count),
        out_shape=(
            jax.ShapeDtypeStruct(self_query.shape, bf16),
            jax.ShapeDtypeStruct(self_query.shape, bf16),
        ),
        in_specs=[vmem] * 11 + [pl.BlockSpec(memory_space=pltpu.SMEM)],
        out_specs=(vmem, vmem),
        scratch_shapes=[
            pltpu.VMEM((wid_count, 2, text_rows, half), bf16),
            pltpu.VMEM((2, text_rows, half), bf16),
            pltpu.VMEM((tokens + 2 * edge, channels), bf16),
            pltpu.VMEM((tokens + 2 * edge, channels), bf16),
            pltpu.VMEM((tokens, depth), f32),
            pltpu.VMEM((tokens, depth), f32),
            pltpu.VMEM((2 * tokens, half), bf16),
            pltpu.VMEM((tokens, half), bf16),
            pltpu.VMEM((2 * tokens, half), f32),
            pltpu.VMEM((half_heads, tokens, depth), bf16),
            pltpu.VMEM((half_heads, tokens, depth), bf16),
            pltpu.VMEM((3, tokens, tokens + 2 * edge), jnp.int32),
            dma((wid_count,)),
            dma((wid_count,)),
            dma((wid_count,)),
            dma,
            dma((4,)),
            dma((4,)),
            dma,
            dma,
            dma((2,)),
            dma((half_heads,)),
            dma((half_heads,)),
        ],
        compiler_params=pltpu.CompilerParams(
            collective_id=0, has_side_effects=True, vmem_limit_bytes=40 * 1024 * 1024
        ),
        name="attention",
    )(
        self_query,
        self_key,
        self_value,
        cross_query,
        text_key,
        text_value,
        image_key,
        image_value,
        query_gain[None],
        key_gain[None],
        cross_gain[None],
        windows,
    )


def solution(mesh):
    in_specs = (
        P("groups", "hgt", "wid", "tp"),
        P("groups", "hgt", "wid", "tp"),
        P("groups", "hgt", "wid", "tp"),
        P("groups", "hgt", "wid", "tp"),
        P(("groups", "wid"), "tp"),
        P(("groups", "wid"), "tp"),
        P("groups", "tp"),
        P("groups", "tp"),
        P("tp"),
        P("tp"),
        P("tp"),
        P("tp", None),
    )
    out_specs = (P("groups", "hgt", "wid", "tp"), P("groups", "hgt", "wid", "tp"))

    def chosen(*args):
        wid_count = mesh.shape["wid"]
        one_row = mesh.shape["hgt"] == 1 and mesh.shape["tp"] == 2
        even = wid_count % 2 == 0 and args[-1].shape[0] % 2 == 0
        if one_row and even:
            return fused_body(wid_count, *args)
        return body(*args)

    return jax.shard_map(chosen, mesh=mesh, in_specs=in_specs, out_specs=out_specs, check_vma=False)
```

```python
import functools
import math

import jax
import jax.numpy as jnp
from jax import lax
from jax.experimental import pallas as pl
from jax.experimental.pallas import tpu as pltpu
from jax.sharding import PartitionSpec as P

TILE = 4


epsilon = 1e-06
masked = -1e30


def padded(value, sides, width):
    for axis, dim in sides:
        count, length = (lax.axis_size(axis), value.shape[dim])
        up = [(i, (i + 1) % count) for i in range(count - 1)]
        down = [(j, i) for i, j in up]
        last = lax.slice_in_dim(value, length - width, length, axis=dim)
        first = lax.slice_in_dim(value, 0, width, axis=dim)
        before = lax.ppermute(last, axis, up)
        after = lax.ppermute(first, axis, down)
        value = jnp.concatenate([before, value, after], axis=dim)
    return value


def grid_positions(frame_count, row_count, col_count, row_start, col_start):
    full_shape = (frame_count, row_count, col_count)
    frame_ids = jnp.arange(frame_count, dtype=jnp.int32)[:, None, None]
    row_ids = jnp.arange(row_count, dtype=jnp.int32)[None, :, None] + row_start
    col_ids = jnp.arange(col_count, dtype=jnp.int32)[None, None, :] + col_start
    return (
        jnp.broadcast_to(frame_ids, full_shape).reshape(-1),
        jnp.broadcast_to(row_ids, full_shape).reshape(-1),
        jnp.broadcast_to(col_ids, full_shape).reshape(-1),
    )


def window_mask(windows, query_pos, key_pos, height_all, width_all):
    inside = (
        (key_pos[1] >= 0) & (key_pos[1] < height_all) & (key_pos[2] >= 0) & (key_pos[2] < width_all)
    )
    frame_gap = jnp.abs(query_pos[0][:, None] - key_pos[0][None, :])
    row_gap = jnp.abs(query_pos[1][:, None] // TILE - key_pos[1][None, :] // TILE)
    col_gap = jnp.abs(query_pos[2][:, None] // TILE - key_pos[2][None, :] // TILE)
    return (
        (frame_gap[None] <= windows[:, 0, None, None])
        & (row_gap[None] <= windows[:, 1, None, None])
        & (col_gap[None] <= windows[:, 2, None, None])
        & inside[None, None, :]
    )


def attend_part(queries, key_rows, value_rows, allowed):
    factor = 1.0 / math.sqrt(queries.shape[-1])
    scores = (
        jnp.einsum("qhd,khd->hqk", queries, key_rows, preferred_element_type=jnp.float32) * factor
    )
    if allowed is not None:
        scores = jnp.where(allowed, scores, masked)
    row_top = jnp.max(scores, axis=-1)
    powers = jnp.exp(scores - row_top[..., None])
    if allowed is not None:
        powers = jnp.where(allowed, powers, 0.0)
    weights = powers.astype(jnp.bfloat16)
    numerator = jnp.einsum("hqk,khd->hqd", weights, value_rows, preferred_element_type=jnp.float32)
    return (row_top, jnp.sum(powers, axis=-1), numerator)


def merge_parts(first, second):
    row_top = jnp.maximum(first[0], second[0])
    upper = jnp.exp(second[0] - row_top)
    return (row_top, second[1] * upper, second[2] * upper[..., None])


def finish_part(part, frame_count, row_count, col_count):
    heads_out = part[2] / part[1][..., None]
    return jnp.transpose(heads_out, (1, 0, 2)).reshape(frame_count, row_count, col_count, -1)


def sum_squares(field):
    wide = field.astype(jnp.float32)
    return jnp.sum(wide * wide, axis=-1)


def apply_norm(field, squares_all, channel_total, gain):
    inverse = lax.rsqrt(squares_all / channel_total + epsilon)
    return (field.astype(jnp.float32) * inverse[..., None] * gain).astype(jnp.bfloat16)


def flat_heads(field, head_count):
    return field.reshape(-1, head_count, field.shape[-1] // head_count)


def body(
    self_query,
    self_key,
    self_value,
    cross_query,
    text_key,
    text_value,
    image_key,
    image_value,
    query_gain,
    key_gain,
    cross_gain,
    windows,
):
    frame_count, row_count, col_count, channels = self_query.shape
    head_count = windows.shape[0]
    channel_total = channels * lax.axis_size("tp")
    height_all = row_count * lax.axis_size("hgt")
    width_all = col_count * lax.axis_size("wid")
    row_start = lax.axis_index("hgt") * row_count
    col_start = lax.axis_index("wid") * col_count
    squares_all = lax.psum(
        (sum_squares(self_query), sum_squares(self_key), sum_squares(cross_query)), "tp"
    )
    q_normed = apply_norm(self_query, squares_all[0], channel_total, query_gain)
    k_normed = apply_norm(self_key, squares_all[1], channel_total, key_gain)
    x_normed = apply_norm(cross_query, squares_all[2], channel_total, cross_gain)
    queries = flat_heads(q_normed, head_count)
    query_pos = grid_positions(frame_count, row_count, col_count, row_start, col_start)
    stacked = jnp.stack((k_normed, self_value))
    extended = padded(stacked, (("wid", 3), ("hgt", 2)), TILE)
    key_pos = grid_positions(
        frame_count, row_count + 2 * TILE, col_count + 2 * TILE, row_start - TILE, col_start - TILE
    )
    allowed = window_mask(windows, query_pos, key_pos, height_all, width_all)
    self_part = attend_part(
        queries, flat_heads(extended[0], head_count), flat_heads(extended[1], head_count), allowed
    )
    self_out = finish_part(self_part, frame_count, row_count, col_count).astype(jnp.bfloat16)
    crosses = flat_heads(x_normed, head_count)
    query_total = crosses.shape[0]
    start_part = (
        jnp.full((head_count, query_total), masked, jnp.float32),
        jnp.zeros((head_count, query_total), jnp.float32),
        jnp.zeros((head_count, query_total, crosses.shape[-1]), jnp.float32),
    )
    fresh = attend_part(
        crosses,
        flat_heads(lax.all_gather(text_key, "wid", axis=0, tiled=True), head_count),
        flat_heads(lax.all_gather(text_value, "wid", axis=0, tiled=True), head_count),
        None,
    )
    text_part = merge_parts(start_part, fresh)
    image_part = attend_part(
        crosses, flat_heads(image_key, head_count), flat_heads(image_value, head_count), None
    )
    cross_out = (
        finish_part(text_part, frame_count, row_count, col_count)
        + finish_part(image_part, frame_count, row_count, col_count)
    ).astype(jnp.bfloat16)
    return (self_out, cross_out)


MESH = pl.DeviceIdType.MESH


def squares_of(ref, head_count, depth, tokens):
    total = jnp.zeros((tokens, depth), jnp.float32)
    for head in range(head_count):
        wide = head_block(ref, head * depth, depth, tokens)
        total = total + wide * wide
    return jnp.sum(total, axis=-1, keepdims=True)


def head_block(ref, start, depth, tokens):
    block = ref[:, :, :, pl.ds(start, depth)]
    return block.astype(jnp.float32).reshape(tokens, depth)


def dot_nt(left, right):
    return lax.dot_general(
        left, right, (((1,), (1,)), ((), ())), preferred_element_type=jnp.float32
    )


def soft_mix(scores, value_rows, factor):
    row_top = jnp.max(scores, axis=-1, keepdims=True)
    powers = jnp.exp((scores - row_top) * factor)
    total = jnp.sum(powers, axis=-1, keepdims=True)
    mixed = jnp.dot(
        powers.astype(jnp.bfloat16), value_rows, preferred_element_type=jnp.float32
    )
    return mixed * (1.0 / total)


def fused(
    wid_count,
    head_count,
    sq_hbm,
    sk_hbm,
    sv_hbm,
    xq_hbm,
    tk_hbm,
    tv_hbm,
    ik_hbm,
    iv_hbm,
    qg_hbm,
    kg_hbm,
    xg_hbm,
    win_ref,
    so_ref,
    co_ref,
    sq_ref,
    sk_ref,
    sv_ref,
    xq_ref,
    ik_ref,
    iv_ref,
    qg_ref,
    kg_ref,
    xg_ref,
    weights,
    totals,
    text,
    text_out,
    keys,
    values,
    stat,
    stat_in,
    cross,
    cross_send,
    image_part,
    back_send,
    back_in,
    gaps,
    local_sem,
    text_recv,
    up_send,
    down_send,
    side_send,
    halo_send,
    halo_recv,
    stat_send,
    stat_recv,
    cross_sem,
    back_send_sem,
    back_recv_sem,
):
    frames, rows, cols, channels = sq_ref.shape
    tokens = frames * rows * cols
    depth = channels // head_count
    half_heads = head_count // 2
    half = half_heads * depth
    edge = frames * rows * TILE
    col_tiles = cols // TILE
    lines = wid_count // 2
    factor = 1.0 / math.sqrt(depth)

    w = lax.axis_index("wid")
    core = lax.axis_index("tp")
    line = w // 2
    side = w % 2
    mate = line * 2 + (1 - side)
    not_first, not_last = w > 0, w < wid_count - 1
    has_down, has_up = line > 0, line < lines - 1

    def at_wid(target):
        return {"wid": target}

    mine = pl.multiple_of(side * half, depth)
    other = pl.multiple_of((1 - side) * half, depth)
    loads = [
        pltpu.make_async_copy(source, target, local_sem.at[at])
        for at, (source, target) in enumerate(
            (
                (tk_hbm.at[:, pl.ds(mine, half)], text.at[0, w]),
                (tk_hbm.at[:, pl.ds(other, half)], text_out.at[0]),
                (tv_hbm.at[:, pl.ds(mine, half)], text.at[1, w]),
                (tv_hbm.at[:, pl.ds(other, half)], text_out.at[1]),
                (sq_hbm, sq_ref),
                (sk_hbm, sk_ref),
                (xq_hbm, xq_ref),
                (sv_hbm, sv_ref),
                (kg_hbm, kg_ref),
                (xg_hbm, xg_ref),
                (qg_hbm, qg_ref),
                (ik_hbm, ik_ref),
                (iv_hbm, iv_ref),
            )
        )
    ]
    for load in loads:
        load.start()

    barrier = pltpu.get_barrier_semaphore()
    pl.semaphore_signal(barrier, inc=1, device_id={"tp": 1 - core}, device_id_type=MESH)
    for cond, target in (
        (not_first, w - 1),
        (not_last, w + 1),
        (has_down, w - 2),
        (has_up, w + 2),
    ):

        @pl.when(cond)
        def _():
            pl.semaphore_signal(barrier, inc=1, device_id=at_wid(target), device_id_type=MESH)

    expected = 1
    for cond in (not_first, not_last, has_down, has_up):
        expected = expected + jnp.where(cond, 1, 0)
    pl.semaphore_wait(barrier, expected)

    def relay(kind, slot, up):
        return pltpu.make_async_remote_copy(
            src_ref=text.at[kind, slot],
            dst_ref=text.at[kind, slot],
            send_sem=(up_send if up else down_send).at[kind, slot],
            recv_sem=text_recv.at[kind, slot],
            device_id=at_wid(w + 2 if up else w - 2),
            device_id_type=MESH,
        )

    def forward(kind, slot, up):
        @pl.when(has_up if up else has_down)
        def _():
            relay(kind, slot, up).start()

    def take(kind, slot):
        pltpu.make_async_remote_copy(
            src_ref=text.at[kind, slot],
            dst_ref=text.at[kind, slot],
            send_sem=side_send.at[kind],
            recv_sem=text_recv.at[kind, slot],
            device_id=at_wid(mate),
            device_id_type=MESH,
        ).wait_recv()

    def relay_step(kind, step, which):
        below, above = (line - step) * 2 + which, (line + step) * 2 + which

        @pl.when(line - step >= 0)
        def _():
            take(kind, below)
            forward(kind, below, True)

        @pl.when(line + step < lines)
        def _():
            take(kind, above)
            forward(kind, above, False)

    steps = [
        (step, side if turn == 0 else 1 - side) for step in range(1, lines - 1) for turn in range(2)
    ]

    def next_step():
        if steps:
            step, which = steps.pop(0)
            for kind in range(2):
                relay_step(kind, step, which)

    side_copies = []
    for kind in range(2):
        loads[2 * kind].wait()
        forward(kind, w, True)
        forward(kind, w, False)
        loads[2 * kind + 1].wait()
        side_copy = pltpu.make_async_remote_copy(
            src_ref=text_out.at[kind],
            dst_ref=text.at[kind, w],
            send_sem=side_send.at[kind],
            recv_sem=text_recv.at[kind, w],
            device_id=at_wid(mate),
            device_id_type=MESH,
        )
        side_copy.start()
        side_copies.append(side_copy)
    for load in loads[4:11]:
        load.wait()

    lane = lax.broadcasted_iota(jnp.int32, (tokens, depth), 1)
    sums = [squares_of(ref, head_count, depth, tokens) for ref in (sq_ref, sk_ref, xq_ref)]
    stat[...] = jnp.where(lane == 0, sums[0], jnp.where(lane == 1, sums[1], sums[2]))
    stat_copy = pltpu.make_async_remote_copy(
        src_ref=stat,
        dst_ref=stat_in,
        send_sem=stat_send,
        recv_sem=stat_recv,
        device_id={"tp": 1 - core},
        device_id_type=MESH,
    )
    stat_copy.start()

    for kind in range(2):
        take(kind, mate)
        forward(kind, mate, True)
        forward(kind, mate, False)

    place = lax.broadcasted_iota(jnp.int32, (tokens, tokens), 0)
    source = lax.broadcasted_iota(jnp.int32, (tokens, tokens), 1)
    inner = lax.rem(place, edge)
    natural = (
        lax.div(inner, rows * TILE) * (rows * cols)
        + lax.rem(lax.div(inner, TILE), rows) * cols
        + lax.div(place, edge) * TILE
        + lax.rem(inner, TILE)
    )
    to_tiles = jnp.where(natural == source, 1.0, 0.0).astype(jnp.bfloat16)

    def tile_order(block):
        return jnp.dot(to_tiles, block, preferred_element_type=jnp.float32).astype(jnp.bfloat16)

    def halo(ref, at, down):
        return pltpu.make_async_remote_copy(
            src_ref=ref.at[pl.ds(edge if down else tokens, edge)],
            dst_ref=ref.at[pl.ds(edge + tokens if down else 0, edge)],
            send_sem=halo_send.at[at],
            recv_sem=halo_recv.at[at],
            device_id=at_wid(w - 1 if down else w + 1),
            device_id_type=MESH,
        )

    def start_halo(ref, at):
        @pl.when(not_first)
        def _():
            halo(ref, at, True).start()

        @pl.when(not_last)
        def _():
            halo(ref, at + 1, False).start()

    @pl.when(w == 0)
    def _():
        for ref in (keys, values):
            ref[0:edge] = jnp.zeros((edge, channels), jnp.bfloat16)

    @pl.when(w == wid_count - 1)
    def _():
        for ref in (keys, values):
            ref[edge + tokens :] = jnp.zeros((edge, channels), jnp.bfloat16)

    for head in range(head_count):
        block = head_block(sv_ref, head * depth, depth, tokens).astype(jnp.bfloat16)
        values[edge : edge + tokens, head * depth : (head + 1) * depth] = tile_order(block)
    start_halo(values, 2)

    stat_copy.wait()
    whole = stat[...] + stat_in[...]
    inverse = lax.rsqrt(whole / (channels * 2) + epsilon)
    inverse_q, inverse_k, inverse_x = inverse[:, 0:1], inverse[:, 1:2], inverse[:, 2:3]

    def normed(ref, gain_ref, start, inverse_of):
        wide = head_block(ref, start, depth, tokens)
        return (wide * inverse_of * gain_ref[pl.ds(start, depth)][None]).astype(jnp.bfloat16)

    for head in range(head_count):
        block = normed(sk_ref, kg_ref, head * depth, inverse_k)
        keys[edge : edge + tokens, head * depth : (head + 1) * depth] = tile_order(block)
    start_halo(keys, 0)
    next_step()

    for head in range(half_heads):
        at = pl.multiple_of((1 - side) * half + head * depth, depth)
        cross_send[:, head * depth : (head + 1) * depth] = normed(xq_ref, xg_ref, at, inverse_x)
    cross_copy = pltpu.make_async_remote_copy(
        src_ref=cross_send,
        dst_ref=cross.at[pl.ds(tokens, tokens)],
        send_sem=cross_sem.at[0],
        recv_sem=cross_sem.at[1],
        device_id=at_wid(mate),
        device_id_type=MESH,
    )
    cross_copy.start()

    for head in range(half_heads):
        at = pl.multiple_of(side * half + head * depth, depth)
        cross[0:tokens, head * depth : (head + 1) * depth] = normed(xq_ref, xg_ref, at, inverse_x)

    spread = (tokens, tokens + 2 * edge)
    query = lax.broadcasted_iota(jnp.int32, spread, 0)
    key = lax.broadcasted_iota(jnp.int32, spread, 1)
    key_tile = lax.div(key, edge) - 1
    key_inner = lax.rem(key, edge)
    key_col = key_tile + w * col_tiles
    inside = (key_col >= 0) & (key_col < wid_count * col_tiles)
    frame_gap = jnp.abs(lax.div(query, rows * cols) - lax.div(key_inner, rows * TILE))
    row_gap = jnp.abs(
        lax.div(lax.rem(lax.div(query, cols), rows), TILE)
        - lax.div(lax.rem(lax.div(key_inner, TILE), rows), TILE)
    )
    col_gap = jnp.abs(lax.div(lax.rem(query, cols), TILE) - key_tile)
    gaps[0] = jnp.where(inside, frame_gap, 1 << 30)
    gaps[1] = row_gap
    gaps[2] = col_gap

    def self_head(head):
        at = slice(head * depth, (head + 1) * depth)
        queries = normed(sq_ref, qg_ref, head * depth, inverse_q)
        scores = dot_nt(queries, keys[:, at])
        allowed = (
            (gaps[0] <= win_ref[0, head])
            & (gaps[1] <= win_ref[1, head])
            & (gaps[2] <= win_ref[2, head])
        )
        mixed = soft_mix(jnp.where(allowed, scores, masked), values[:, at], factor)
        so_ref[:, :, :, at] = mixed.reshape(frames, rows, cols, depth).astype(jnp.bfloat16)

    def image_head(head):
        at = slice(head * depth, (head + 1) * depth)
        there = pl.ds(pl.multiple_of(side * half + head * depth, depth), depth)
        scores = dot_nt(cross[:, at], ik_ref[:, there])
        image_part[:, at] = soft_mix(scores, iv_ref[:, there], factor)

    next_step()
    cross_copy.wait_recv()
    loads[11].wait()
    loads[12].wait()
    for head in range(half_heads):
        image_head(head)
        if head == half_heads // 2 - 1:
            next_step()
    while steps:
        next_step()

    def wait_halo(ref, at):
        @pl.when(not_last)
        def _():
            halo(ref, at, True).wait_recv()

        @pl.when(not_first)
        def _():
            halo(ref, at + 1, False).wait_recv()

    wait_halo(values, 2)
    wait_halo(keys, 0)
    for head in range(head_count):
        self_head(head)

    def last_step(kind):
        if lines > 1:
            for which in range(2):
                relay_step(kind, lines - 1, which)

    rows_all = wid_count * tk_hbm.shape[0]
    last_step(0)
    for head in range(half_heads):
        at = slice(head * depth, (head + 1) * depth)
        scores = dot_nt(cross[:, at], text[0, :, :, at].reshape(rows_all, depth))
        row_top = jnp.max(scores, axis=-1, keepdims=True)
        powers = jnp.exp((scores - row_top) * factor)
        total = jnp.sum(powers, axis=-1, keepdims=True)
        totals[:, at] = jnp.broadcast_to(1.0 / total, (2 * tokens, depth))
        weights[head] = powers.astype(jnp.bfloat16)
    last_step(1)
    backs = []
    for head in range(half_heads):
        at = slice(head * depth, (head + 1) * depth)
        mixed = jnp.dot(
            weights[head],
            text[1, :, :, at].reshape(rows_all, depth),
            preferred_element_type=jnp.float32,
        )
        mixed = mixed * totals[:, at]
        mixed = mixed + image_part[:, at]
        back_send[head] = mixed[tokens:].astype(jnp.bfloat16)
        back = pltpu.make_async_remote_copy(
            src_ref=back_send.at[head],
            dst_ref=back_in.at[head],
            send_sem=back_send_sem.at[head],
            recv_sem=back_recv_sem.at[head],
            device_id=at_wid(mate),
            device_id_type=MESH,
        )
        back.start()
        backs.append(back)
        there = pl.ds(pl.multiple_of(side * half + head * depth, depth), depth)
        own = mixed[:tokens].reshape(frames, rows, cols, depth)
        co_ref[:, :, :, there] = own.astype(jnp.bfloat16)

    for side_copy in side_copies:
        side_copy.wait_send()
    cross_copy.wait_send()
    for at, ref in ((0, keys), (2, values)):

        @pl.when(not_first)
        def _():
            halo(ref, at, True).wait_send()

        @pl.when(not_last)
        def _():
            halo(ref, at + 1, False).wait_send()

    for place_line in range(lines):
        for place_side in range(2):
            slot = place_line * 2 + place_side

            @pl.when(has_up & (place_line <= line))
            def _():
                relay(0, slot, True).wait_send()
                relay(1, slot, True).wait_send()

            @pl.when(has_down & (place_line >= line))
            def _():
                relay(0, slot, False).wait_send()
                relay(1, slot, False).wait_send()

    for head in range(half_heads):
        backs[head].wait()
        there = pl.ds(pl.multiple_of((1 - side) * half + head * depth, depth), depth)
        came = back_in[head].astype(jnp.float32).reshape(frames, rows, cols, depth)
        co_ref[:, :, :, there] = came.astype(jnp.bfloat16)


def fused_body(
    wid_count,
    self_query,
    self_key,
    self_value,
    cross_query,
    text_key,
    text_value,
    image_key,
    image_value,
    query_gain,
    key_gain,
    cross_gain,
    windows,
):
    frames, rows, cols, channels = self_query.shape
    tokens = frames * rows * cols
    head_count = windows.shape[0]
    depth = channels // head_count
    half_heads = head_count // 2
    half = half_heads * depth
    edge = frames * rows * TILE
    text_rows = text_key.shape[0]
    bf16, f32 = jnp.bfloat16, jnp.float32
    dma = pltpu.SemaphoreType.DMA
    vmem = pl.BlockSpec(memory_space=pltpu.VMEM)
    return pl.pallas_call(
        functools.partial(fused, wid_count, head_count),
        out_shape=(
            jax.ShapeDtypeStruct(self_query.shape, bf16),
            jax.ShapeDtypeStruct(self_query.shape, bf16),
        ),
        in_specs=[pl.BlockSpec(memory_space=pltpu.HBM)] * 11 + [pl.BlockSpec(memory_space=pltpu.SMEM)],
        out_specs=(vmem, vmem),
        scratch_shapes=[
            *[pltpu.VMEM(self_query.shape, bf16)] * 4,
            *[pltpu.VMEM(image_key.shape, bf16)] * 2,
            *[pltpu.VMEM((channels,), f32)] * 3,
            pltpu.VMEM((half_heads, 2 * tokens, wid_count * text_rows), bf16),
            pltpu.VMEM((2 * tokens, half), f32),
            pltpu.VMEM((2, wid_count, text_rows, half), bf16),
            pltpu.VMEM((2, text_rows, half), bf16),
            pltpu.VMEM((tokens + 2 * edge, channels), bf16),
            pltpu.VMEM((tokens + 2 * edge, channels), bf16),
            pltpu.VMEM((tokens, depth), f32),
            pltpu.VMEM((tokens, depth), f32),
            pltpu.VMEM((2 * tokens, half), bf16),
            pltpu.VMEM((tokens, half), bf16),
            pltpu.VMEM((2 * tokens, half), f32),
            pltpu.VMEM((half_heads, tokens, depth), bf16),
            pltpu.VMEM((half_heads, tokens, depth), bf16),
            pltpu.VMEM((3, tokens, tokens + 2 * edge), jnp.int32),
            dma((13,)),
            dma((2, wid_count)),
            dma((2, wid_count)),
            dma((2, wid_count)),
            dma((2,)),
            dma((4,)),
            dma((4,)),
            dma,
            dma,
            dma((2,)),
            dma((half_heads,)),
            dma((half_heads,)),
        ],
        compiler_params=pltpu.CompilerParams(
            collective_id=0, has_side_effects=True, vmem_limit_bytes=56 * 1024 * 1024
        ),
        name="attention",
    )(
        self_query,
        self_key,
        self_value,
        cross_query,
        text_key,
        text_value,
        image_key,
        image_value,
        query_gain,
        key_gain,
        cross_gain,
        windows.T,
    )


def solution(mesh):
    in_specs = (
        P("groups", "hgt", "wid", "tp"),
        P("groups", "hgt", "wid", "tp"),
        P("groups", "hgt", "wid", "tp"),
        P("groups", "hgt", "wid", "tp"),
        P(("groups", "wid"), "tp"),
        P(("groups", "wid"), "tp"),
        P("groups", "tp"),
        P("groups", "tp"),
        P("tp"),
        P("tp"),
        P("tp"),
        P("tp", None),
    )
    out_specs = (P("groups", "hgt", "wid", "tp"), P("groups", "hgt", "wid", "tp"))

    def chosen(*args):
        wid_count = mesh.shape["wid"]
        one_row = mesh.shape["hgt"] == 1 and mesh.shape["tp"] == 2
        even = wid_count % 2 == 0 and args[-1].shape[0] % 2 == 0
        if one_row and even:
            return fused_body(wid_count, *args)
        return body(*args)

    return jax.shard_map(chosen, mesh=mesh, in_specs=in_specs, out_specs=out_specs, check_vma=False)
```

```python
import functools
import math

import jax
import jax.numpy as jnp
from jax import lax
from jax.experimental import pallas as pl
from jax.experimental.pallas import tpu as pltpu
from jax.sharding import PartitionSpec as P

TILE = 4


epsilon = 1e-06
masked = -1e30


def padded(value, sides, width):
    for axis, dim in sides:
        count, length = (lax.axis_size(axis), value.shape[dim])
        up = [(i, (i + 1) % count) for i in range(count - 1)]
        down = [(j, i) for i, j in up]
        last = lax.slice_in_dim(value, length - width, length, axis=dim)
        first = lax.slice_in_dim(value, 0, width, axis=dim)
        before = lax.ppermute(last, axis, up)
        after = lax.ppermute(first, axis, down)
        value = jnp.concatenate([before, value, after], axis=dim)
    return value


def grid_positions(frame_count, row_count, col_count, row_start, col_start):
    full_shape = (frame_count, row_count, col_count)
    frame_ids = jnp.arange(frame_count, dtype=jnp.int32)[:, None, None]
    row_ids = jnp.arange(row_count, dtype=jnp.int32)[None, :, None] + row_start
    col_ids = jnp.arange(col_count, dtype=jnp.int32)[None, None, :] + col_start
    return (
        jnp.broadcast_to(frame_ids, full_shape).reshape(-1),
        jnp.broadcast_to(row_ids, full_shape).reshape(-1),
        jnp.broadcast_to(col_ids, full_shape).reshape(-1),
    )


def window_mask(windows, query_pos, key_pos, height_all, width_all):
    inside = (
        (key_pos[1] >= 0) & (key_pos[1] < height_all) & (key_pos[2] >= 0) & (key_pos[2] < width_all)
    )
    frame_gap = jnp.abs(query_pos[0][:, None] - key_pos[0][None, :])
    row_gap = jnp.abs(query_pos[1][:, None] // TILE - key_pos[1][None, :] // TILE)
    col_gap = jnp.abs(query_pos[2][:, None] // TILE - key_pos[2][None, :] // TILE)
    return (
        (frame_gap[None] <= windows[:, 0, None, None])
        & (row_gap[None] <= windows[:, 1, None, None])
        & (col_gap[None] <= windows[:, 2, None, None])
        & inside[None, None, :]
    )


def attend_part(queries, key_rows, value_rows, allowed):
    factor = 1.0 / math.sqrt(queries.shape[-1])
    scores = (
        jnp.einsum("qhd,khd->hqk", queries, key_rows, preferred_element_type=jnp.float32) * factor
    )
    if allowed is not None:
        scores = jnp.where(allowed, scores, masked)
    row_top = jnp.max(scores, axis=-1)
    powers = jnp.exp(scores - row_top[..., None])
    if allowed is not None:
        powers = jnp.where(allowed, powers, 0.0)
    weights = powers.astype(jnp.bfloat16)
    numerator = jnp.einsum("hqk,khd->hqd", weights, value_rows, preferred_element_type=jnp.float32)
    return (row_top, jnp.sum(powers, axis=-1), numerator)


def merge_parts(first, second):
    row_top = jnp.maximum(first[0], second[0])
    upper = jnp.exp(second[0] - row_top)
    return (row_top, second[1] * upper, second[2] * upper[..., None])


def finish_part(part, frame_count, row_count, col_count):
    heads_out = part[2] / part[1][..., None]
    return jnp.transpose(heads_out, (1, 0, 2)).reshape(frame_count, row_count, col_count, -1)


def sum_squares(field):
    wide = field.astype(jnp.float32)
    return jnp.sum(wide * wide, axis=-1)


def apply_norm(field, squares_all, channel_total, gain):
    inverse = lax.rsqrt(squares_all / channel_total + epsilon)
    return (field.astype(jnp.float32) * inverse[..., None] * gain).astype(jnp.bfloat16)


def flat_heads(field, head_count):
    return field.reshape(-1, head_count, field.shape[-1] // head_count)


def body(
    self_query,
    self_key,
    self_value,
    cross_query,
    text_key,
    text_value,
    image_key,
    image_value,
    query_gain,
    key_gain,
    cross_gain,
    windows,
):
    frame_count, row_count, col_count, channels = self_query.shape
    head_count = windows.shape[0]
    channel_total = channels * lax.axis_size("tp")
    height_all = row_count * lax.axis_size("hgt")
    width_all = col_count * lax.axis_size("wid")
    row_start = lax.axis_index("hgt") * row_count
    col_start = lax.axis_index("wid") * col_count
    squares_all = lax.psum(
        (sum_squares(self_query), sum_squares(self_key), sum_squares(cross_query)), "tp"
    )
    q_normed = apply_norm(self_query, squares_all[0], channel_total, query_gain)
    k_normed = apply_norm(self_key, squares_all[1], channel_total, key_gain)
    x_normed = apply_norm(cross_query, squares_all[2], channel_total, cross_gain)
    queries = flat_heads(q_normed, head_count)
    query_pos = grid_positions(frame_count, row_count, col_count, row_start, col_start)
    stacked = jnp.stack((k_normed, self_value))
    extended = padded(stacked, (("wid", 3), ("hgt", 2)), TILE)
    key_pos = grid_positions(
        frame_count, row_count + 2 * TILE, col_count + 2 * TILE, row_start - TILE, col_start - TILE
    )
    allowed = window_mask(windows, query_pos, key_pos, height_all, width_all)
    self_part = attend_part(
        queries, flat_heads(extended[0], head_count), flat_heads(extended[1], head_count), allowed
    )
    self_out = finish_part(self_part, frame_count, row_count, col_count).astype(jnp.bfloat16)
    crosses = flat_heads(x_normed, head_count)
    query_total = crosses.shape[0]
    start_part = (
        jnp.full((head_count, query_total), masked, jnp.float32),
        jnp.zeros((head_count, query_total), jnp.float32),
        jnp.zeros((head_count, query_total, crosses.shape[-1]), jnp.float32),
    )
    fresh = attend_part(
        crosses,
        flat_heads(lax.all_gather(text_key, "wid", axis=0, tiled=True), head_count),
        flat_heads(lax.all_gather(text_value, "wid", axis=0, tiled=True), head_count),
        None,
    )
    text_part = merge_parts(start_part, fresh)
    image_part = attend_part(
        crosses, flat_heads(image_key, head_count), flat_heads(image_value, head_count), None
    )
    cross_out = (
        finish_part(text_part, frame_count, row_count, col_count)
        + finish_part(image_part, frame_count, row_count, col_count)
    ).astype(jnp.bfloat16)
    return (self_out, cross_out)


MESH = pl.DeviceIdType.MESH
GUESTS = 2


def squares_of(ref, head_count, depth, tokens):
    total = jnp.zeros((tokens, depth), jnp.float32)
    for head in range(head_count):
        wide = head_block(ref, head * depth, depth, tokens)
        total = total + wide * wide
    return jnp.sum(total, axis=-1, keepdims=True)


def head_block(ref, start, depth, tokens):
    block = ref[:, :, :, pl.ds(start, depth)]
    return block.astype(jnp.float32).reshape(tokens, depth)


def dot_nt(left, right):
    return lax.dot_general(
        left, right, (((1,), (1,)), ((), ())), preferred_element_type=jnp.float32
    )


def soft_mix(scores, value_rows, factor):
    row_top = jnp.max(scores, axis=-1, keepdims=True)
    powers = jnp.exp((scores - row_top) * factor)
    total = jnp.sum(powers, axis=-1, keepdims=True)
    mixed = jnp.dot(
        powers.astype(jnp.bfloat16), value_rows, preferred_element_type=jnp.float32
    )
    return mixed * (1.0 / total)


def guest_heads(wid_count, half_heads):
    return GUESTS if wid_count >= 8 and half_heads > GUESTS else 0


def fused(
    wid_count,
    head_count,
    sq_hbm,
    sk_hbm,
    sv_hbm,
    xq_hbm,
    tk_hbm,
    tv_hbm,
    ik_hbm,
    iv_hbm,
    qg_hbm,
    kg_hbm,
    xg_hbm,
    win_ref,
    so_ref,
    co_ref,
    sq_ref,
    sk_ref,
    sv_ref,
    xq_ref,
    ik_ref,
    iv_ref,
    qg_ref,
    kg_ref,
    xg_ref,
    weights,
    totals,
    guest_in,
    guest_out,
    guest_sem,
    text,
    text_out,
    keys,
    values,
    stat,
    stat_in,
    cross,
    cross_send,
    image_part,
    back_send,
    back_in,
    gaps,
    local_sem,
    text_recv,
    up_send,
    down_send,
    side_send,
    halo_send,
    halo_recv,
    stat_send,
    stat_recv,
    cross_sem,
    back_send_sem,
    back_recv_sem,
):
    frames, rows, cols, channels = sq_ref.shape
    tokens = frames * rows * cols
    depth = channels // head_count
    half_heads = head_count // 2
    half = half_heads * depth
    edge = frames * rows * TILE
    col_tiles = cols // TILE
    lines = wid_count // 2
    factor = 1.0 / math.sqrt(depth)
    guests = guest_heads(wid_count, half_heads)
    kept = half - guests * depth

    w = lax.axis_index("wid")
    core = lax.axis_index("tp")
    line = w // 2
    side = w % 2
    mate = line * 2 + (1 - side)
    not_first, not_last = w > 0, w < wid_count - 1
    has_down, has_up = line > 0, line < lines - 1
    is_end = (line == 0) | (line == lines - 1)
    is_host = (line == 1) | (line == lines - 2)
    guest_peer = w + jnp.where((line == 0) | (line == lines - 2), 2, -2)

    def at_wid(target):
        return {"wid": target}

    mine = pl.multiple_of(side * half, depth)
    other = pl.multiple_of((1 - side) * half, depth)
    loads = [
        pltpu.make_async_copy(source, target, local_sem.at[at])
        for at, (source, target) in enumerate(
            (
                (tk_hbm.at[:, pl.ds(mine, half)], text.at[0, w]),
                (tk_hbm.at[:, pl.ds(other, half)], text_out.at[0]),
                (tv_hbm.at[:, pl.ds(mine, half)], text.at[1, w]),
                (tv_hbm.at[:, pl.ds(other, half)], text_out.at[1]),
                (sq_hbm, sq_ref),
                (sk_hbm, sk_ref),
                (xq_hbm, xq_ref),
                (sv_hbm, sv_ref),
                (kg_hbm, kg_ref),
                (xg_hbm, xg_ref),
                (qg_hbm, qg_ref),
                (ik_hbm, ik_ref),
                (iv_hbm, iv_ref),
            )
        )
    ]
    for load in loads:
        load.start()

    barrier = pltpu.get_barrier_semaphore()
    pl.semaphore_signal(barrier, inc=1, device_id={"tp": 1 - core}, device_id_type=MESH)
    for cond, target in (
        (not_first, w - 1),
        (not_last, w + 1),
        (has_down, w - 2),
        (has_up, w + 2),
    ):

        @pl.when(cond)
        def _():
            pl.semaphore_signal(barrier, inc=1, device_id=at_wid(target), device_id_type=MESH)

    expected = 1
    for cond in (not_first, not_last, has_down, has_up):
        expected = expected + jnp.where(cond, 1, 0)
    pl.semaphore_wait(barrier, expected)

    def slot_of(kind, slot, part):
        if part:
            return text.at[kind, slot, :, pl.ds(0, kept)]
        return text.at[kind, slot]

    def relay(kind, slot, up, part):
        return pltpu.make_async_remote_copy(
            src_ref=slot_of(kind, slot, part),
            dst_ref=slot_of(kind, slot, part),
            send_sem=(up_send if up else down_send).at[kind, slot],
            recv_sem=text_recv.at[kind, slot],
            device_id=at_wid(w + 2 if up else w - 2),
            device_id_type=MESH,
        )

    def with_relay(kind, slot, up, cond, act):
        cond = cond & (has_up if up else has_down)
        if guests == 0:
            pl.when(cond)(lambda: act(relay(kind, slot, up, False)))
            return
        near = (line == lines - 2) if up else (line == 1)
        pl.when(cond & near)(lambda: act(relay(kind, slot, up, True)))
        pl.when(cond & jnp.logical_not(near))(lambda: act(relay(kind, slot, up, False)))

    def forward(kind, slot, up):
        with_relay(kind, slot, up, w >= 0, lambda copy: copy.start())

    def take(kind, slot, part=False):
        pltpu.make_async_remote_copy(
            src_ref=slot_of(kind, slot, part),
            dst_ref=slot_of(kind, slot, part),
            send_sem=side_send.at[kind],
            recv_sem=text_recv.at[kind, slot],
            device_id=at_wid(mate),
            device_id_type=MESH,
        ).wait_recv()

    def take_line(kind, slot):
        if guests == 0:
            take(kind, slot)
            return
        pl.when(is_end)(lambda: take(kind, slot, True))
        pl.when(jnp.logical_not(is_end))(lambda: take(kind, slot))

    def relay_step(kind, step, which):
        below, above = (line - step) * 2 + which, (line + step) * 2 + which

        @pl.when(line - step >= 0)
        def _():
            take_line(kind, below)
            forward(kind, below, True)

        @pl.when(line + step < lines)
        def _():
            take_line(kind, above)
            forward(kind, above, False)

    steps = [
        (step, side if turn == 0 else 1 - side) for step in range(1, lines - 1) for turn in range(2)
    ]

    def next_step():
        if steps:
            step, which = steps.pop(0)
            for kind in range(2):
                relay_step(kind, step, which)

    side_copies = []
    for kind in range(2):
        loads[2 * kind].wait()
        forward(kind, w, True)
        forward(kind, w, False)
        loads[2 * kind + 1].wait()
        side_copy = pltpu.make_async_remote_copy(
            src_ref=text_out.at[kind],
            dst_ref=text.at[kind, w],
            send_sem=side_send.at[kind],
            recv_sem=text_recv.at[kind, w],
            device_id=at_wid(mate),
            device_id_type=MESH,
        )
        side_copy.start()
        side_copies.append(side_copy)
    for load in loads[4:11]:
        load.wait()

    lane = lax.broadcasted_iota(jnp.int32, (tokens, depth), 1)
    sums = [squares_of(ref, head_count, depth, tokens) for ref in (sq_ref, sk_ref, xq_ref)]
    stat[...] = jnp.where(lane == 0, sums[0], jnp.where(lane == 1, sums[1], sums[2]))
    stat_copy = pltpu.make_async_remote_copy(
        src_ref=stat,
        dst_ref=stat_in,
        send_sem=stat_send,
        recv_sem=stat_recv,
        device_id={"tp": 1 - core},
        device_id_type=MESH,
    )
    stat_copy.start()

    for kind in range(2):
        take(kind, mate)
        forward(kind, mate, True)
        forward(kind, mate, False)

    place = lax.broadcasted_iota(jnp.int32, (tokens, tokens), 0)
    source = lax.broadcasted_iota(jnp.int32, (tokens, tokens), 1)
    inner = lax.rem(place, edge)
    natural = (
        lax.div(inner, rows * TILE) * (rows * cols)
        + lax.rem(lax.div(inner, TILE), rows) * cols
        + lax.div(place, edge) * TILE
        + lax.rem(inner, TILE)
    )
    to_tiles = jnp.where(natural == source, 1.0, 0.0).astype(jnp.bfloat16)

    def tile_order(block):
        return jnp.dot(to_tiles, block, preferred_element_type=jnp.float32).astype(jnp.bfloat16)

    def halo(ref, at, down):
        return pltpu.make_async_remote_copy(
            src_ref=ref.at[pl.ds(edge if down else tokens, edge)],
            dst_ref=ref.at[pl.ds(edge + tokens if down else 0, edge)],
            send_sem=halo_send.at[at],
            recv_sem=halo_recv.at[at],
            device_id=at_wid(w - 1 if down else w + 1),
            device_id_type=MESH,
        )

    def start_halo(ref, at):
        @pl.when(not_first)
        def _():
            halo(ref, at, True).start()

        @pl.when(not_last)
        def _():
            halo(ref, at + 1, False).start()

    @pl.when(w == 0)
    def _():
        for ref in (keys, values):
            ref[0:edge] = jnp.zeros((edge, channels), jnp.bfloat16)

    @pl.when(w == wid_count - 1)
    def _():
        for ref in (keys, values):
            ref[edge + tokens :] = jnp.zeros((edge, channels), jnp.bfloat16)

    for head in range(head_count):
        block = head_block(sv_ref, head * depth, depth, tokens).astype(jnp.bfloat16)
        values[edge : edge + tokens, head * depth : (head + 1) * depth] = tile_order(block)
    start_halo(values, 2)

    stat_copy.wait()
    whole = stat[...] + stat_in[...]
    inverse = lax.rsqrt(whole / (channels * 2) + epsilon)
    inverse_q, inverse_k, inverse_x = inverse[:, 0:1], inverse[:, 1:2], inverse[:, 2:3]

    def normed(ref, gain_ref, start, inverse_of):
        wide = head_block(ref, start, depth, tokens)
        return (wide * inverse_of * gain_ref[pl.ds(start, depth)][None]).astype(jnp.bfloat16)

    for head in range(head_count):
        block = normed(sk_ref, kg_ref, head * depth, inverse_k)
        keys[edge : edge + tokens, head * depth : (head + 1) * depth] = tile_order(block)
    start_halo(keys, 0)
    next_step()

    for head in range(half_heads):
        at = pl.multiple_of((1 - side) * half + head * depth, depth)
        cross_send[:, head * depth : (head + 1) * depth] = normed(xq_ref, xg_ref, at, inverse_x)
    cross_copy = pltpu.make_async_remote_copy(
        src_ref=cross_send,
        dst_ref=cross.at[pl.ds(tokens, tokens)],
        send_sem=cross_sem.at[0],
        recv_sem=cross_sem.at[1],
        device_id=at_wid(mate),
        device_id_type=MESH,
    )
    cross_copy.start()

    for head in range(half_heads):
        at = pl.multiple_of(side * half + head * depth, depth)
        cross[0:tokens, head * depth : (head + 1) * depth] = normed(xq_ref, xg_ref, at, inverse_x)

    spread = (tokens, tokens + 2 * edge)
    query = lax.broadcasted_iota(jnp.int32, spread, 0)
    key = lax.broadcasted_iota(jnp.int32, spread, 1)
    key_tile = lax.div(key, edge) - 1
    key_inner = lax.rem(key, edge)
    key_col = key_tile + w * col_tiles
    inside = (key_col >= 0) & (key_col < wid_count * col_tiles)
    frame_gap = jnp.abs(lax.div(query, rows * cols) - lax.div(key_inner, rows * TILE))
    row_gap = jnp.abs(
        lax.div(lax.rem(lax.div(query, cols), rows), TILE)
        - lax.div(lax.rem(lax.div(key_inner, TILE), rows), TILE)
    )
    col_gap = jnp.abs(lax.div(lax.rem(query, cols), TILE) - key_tile)
    gaps[0] = jnp.where(inside, frame_gap, 1 << 30)
    gaps[1] = row_gap
    gaps[2] = col_gap

    def self_head(head):
        at = slice(head * depth, (head + 1) * depth)
        queries = normed(sq_ref, qg_ref, head * depth, inverse_q)
        scores = dot_nt(queries, keys[:, at])
        allowed = (
            (gaps[0] <= win_ref[0, head])
            & (gaps[1] <= win_ref[1, head])
            & (gaps[2] <= win_ref[2, head])
        )
        mixed = soft_mix(jnp.where(allowed, scores, masked), values[:, at], factor)
        so_ref[:, :, :, at] = mixed.reshape(frames, rows, cols, depth).astype(jnp.bfloat16)

    def image_head(head):
        at = slice(head * depth, (head + 1) * depth)
        there = pl.ds(pl.multiple_of(side * half + head * depth, depth), depth)
        scores = dot_nt(cross[:, at], ik_ref[:, there])
        image_part[:, at] = soft_mix(scores, iv_ref[:, there], factor)

    next_step()
    cross_copy.wait_recv()

    def guest_copy(result):
        return pltpu.make_async_remote_copy(
            src_ref=guest_out if result else cross.at[:, pl.ds(kept, guests * depth)],
            dst_ref=guest_in,
            send_sem=guest_sem.at[2 if result else 0],
            recv_sem=guest_sem.at[3 if result else 1],
            device_id=at_wid(guest_peer),
            device_id_type=MESH,
        )

    if guests:
        pl.when(is_end)(lambda: guest_copy(False).start())
    loads[11].wait()
    loads[12].wait()
    for head in range(half_heads):
        image_head(head)
        if head == half_heads // 2 - 1:
            next_step()
    while steps:
        next_step()

    def wait_halo(ref, at):
        @pl.when(not_last)
        def _():
            halo(ref, at, True).wait_recv()

        @pl.when(not_first)
        def _():
            halo(ref, at + 1, False).wait_recv()

    wait_halo(values, 2)
    wait_halo(keys, 0)
    for head in range(head_count):
        self_head(head)

    def last_step(kind):
        if lines > 1:
            for which in range(2):
                relay_step(kind, lines - 1, which)

    rows_all = wid_count * tk_hbm.shape[0]
    def text_weights(queries, at):
        scores = dot_nt(queries, text[0, :, :, at].reshape(rows_all, depth))
        row_top = jnp.max(scores, axis=-1, keepdims=True)
        powers = jnp.exp((scores - row_top) * factor)
        total = jnp.sum(powers, axis=-1, keepdims=True)
        return powers.astype(jnp.bfloat16), 1.0 / total

    def text_mix(shares, at):
        return jnp.dot(
            shares,
            text[1, :, :, at].reshape(rows_all, depth),
            preferred_element_type=jnp.float32,
        )

    def columns(head):
        return slice(head * depth, (head + 1) * depth)

    def weigh(head):
        at = columns(head)
        shares, inverse_total = text_weights(cross[:, at], at)
        totals[:, at] = jnp.broadcast_to(inverse_total, (2 * tokens, depth))
        weights[head] = shares

    def back(head):
        return pltpu.make_async_remote_copy(
            src_ref=back_send.at[head],
            dst_ref=back_in.at[head],
            send_sem=back_send_sem.at[head],
            recv_sem=back_recv_sem.at[head],
            device_id=at_wid(mate),
            device_id_type=MESH,
        )

    def give(head, mixed):
        back_send[head] = mixed[tokens:].astype(jnp.bfloat16)
        back(head).start()
        there = pl.ds(pl.multiple_of(side * half + head * depth, depth), depth)
        own = mixed[:tokens].astype(jnp.float32).reshape(frames, rows, cols, depth)
        co_ref[:, :, :, there] = own.astype(jnp.bfloat16)

    def mix(head):
        at = columns(head)
        give(head, text_mix(weights[head], at) * totals[:, at] + image_part[:, at])

    kept_heads = half_heads - guests
    last_step(0)
    for head in range(kept_heads):
        weigh(head)
    if guests:

        @pl.when(jnp.logical_not(is_end))
        def _():
            for head in range(kept_heads, half_heads):
                weigh(head)

    last_step(1)
    if guests:

        @pl.when(is_host)
        def _():
            guest_copy(False).wait_recv()
            for guest in range(guests):
                at = columns(kept_heads + guest)
                queries = guest_in[:, columns(guest)]
                shares, inverse_total = text_weights(queries, at)
                mixed = text_mix(shares, at) * inverse_total
                first = side * half + (kept_heads + guest) * depth
                there = pl.ds(pl.multiple_of(first, depth), depth)
                scores = dot_nt(queries, ik_ref[:, there])
                mixed = mixed + soft_mix(scores, iv_ref[:, there], factor)
                guest_out[:, columns(guest)] = mixed.astype(jnp.bfloat16)
            guest_copy(True).start()

    for head in range(kept_heads):
        mix(head)
    if guests:

        @pl.when(jnp.logical_not(is_end))
        def _():
            for head in range(kept_heads, half_heads):
                mix(head)

        @pl.when(is_end)
        def _():
            guest_copy(True).wait_recv()
            for guest in range(guests):
                give(kept_heads + guest, guest_in[:, columns(guest)])
            guest_copy(False).wait_send()

        @pl.when(is_host)
        def _():
            guest_copy(True).wait_send()

    for side_copy in side_copies:
        side_copy.wait_send()
    cross_copy.wait_send()
    for at, ref in ((0, keys), (2, values)):

        @pl.when(not_first)
        def _():
            halo(ref, at, True).wait_send()

        @pl.when(not_last)
        def _():
            halo(ref, at + 1, False).wait_send()

    for place_line in range(lines):
        for place_side in range(2):
            slot = place_line * 2 + place_side

            for kind in range(2):
                with_relay(kind, slot, True, place_line <= line, lambda copy: copy.wait_send())
                with_relay(kind, slot, False, place_line >= line, lambda copy: copy.wait_send())

    for head in range(half_heads):
        back(head).wait()
        there = pl.ds(pl.multiple_of((1 - side) * half + head * depth, depth), depth)
        came = back_in[head].astype(jnp.float32).reshape(frames, rows, cols, depth)
        co_ref[:, :, :, there] = came.astype(jnp.bfloat16)


def fused_body(
    wid_count,
    self_query,
    self_key,
    self_value,
    cross_query,
    text_key,
    text_value,
    image_key,
    image_value,
    query_gain,
    key_gain,
    cross_gain,
    windows,
):
    frames, rows, cols, channels = self_query.shape
    tokens = frames * rows * cols
    head_count = windows.shape[0]
    depth = channels // head_count
    half_heads = head_count // 2
    half = half_heads * depth
    edge = frames * rows * TILE
    text_rows = text_key.shape[0]
    guests = guest_heads(wid_count, half_heads)
    bf16, f32 = jnp.bfloat16, jnp.float32
    dma = pltpu.SemaphoreType.DMA
    vmem = pl.BlockSpec(memory_space=pltpu.VMEM)
    return pl.pallas_call(
        functools.partial(fused, wid_count, head_count),
        out_shape=(
            jax.ShapeDtypeStruct(self_query.shape, bf16),
            jax.ShapeDtypeStruct(self_query.shape, bf16),
        ),
        in_specs=[pl.BlockSpec(memory_space=pltpu.HBM)] * 11 + [pl.BlockSpec(memory_space=pltpu.SMEM)],
        out_specs=(vmem, vmem),
        scratch_shapes=[
            *[pltpu.VMEM(self_query.shape, bf16)] * 4,
            *[pltpu.VMEM(image_key.shape, bf16)] * 2,
            *[pltpu.VMEM((channels,), f32)] * 3,
            pltpu.VMEM((half_heads, 2 * tokens, wid_count * text_rows), bf16),
            pltpu.VMEM((2 * tokens, half), f32),
            *[pltpu.VMEM((2 * tokens, max(guests, 1) * depth), bf16)] * 2,
            dma((4,)),
            pltpu.VMEM((2, wid_count, text_rows, half), bf16),
            pltpu.VMEM((2, text_rows, half), bf16),
            pltpu.VMEM((tokens + 2 * edge, channels), bf16),
            pltpu.VMEM((tokens + 2 * edge, channels), bf16),
            pltpu.VMEM((tokens, depth), f32),
            pltpu.VMEM((tokens, depth), f32),
            pltpu.VMEM((2 * tokens, half), bf16),
            pltpu.VMEM((tokens, half), bf16),
            pltpu.VMEM((2 * tokens, half), f32),
            pltpu.VMEM((half_heads, tokens, depth), bf16),
            pltpu.VMEM((half_heads, tokens, depth), bf16),
            pltpu.VMEM((3, tokens, tokens + 2 * edge), jnp.int32),
            dma((13,)),
            dma((2, wid_count)),
            dma((2, wid_count)),
            dma((2, wid_count)),
            dma((2,)),
            dma((4,)),
            dma((4,)),
            dma,
            dma,
            dma((2,)),
            dma((half_heads,)),
            dma((half_heads,)),
        ],
        compiler_params=pltpu.CompilerParams(
            collective_id=0, has_side_effects=True, vmem_limit_bytes=56 * 1024 * 1024
        ),
        name="attention",
    )(
        self_query,
        self_key,
        self_value,
        cross_query,
        text_key,
        text_value,
        image_key,
        image_value,
        query_gain,
        key_gain,
        cross_gain,
        windows.T,
    )


def solution(mesh):
    in_specs = (
        P("groups", "hgt", "wid", "tp"),
        P("groups", "hgt", "wid", "tp"),
        P("groups", "hgt", "wid", "tp"),
        P("groups", "hgt", "wid", "tp"),
        P(("groups", "wid"), "tp"),
        P(("groups", "wid"), "tp"),
        P("groups", "tp"),
        P("groups", "tp"),
        P("tp"),
        P("tp"),
        P("tp"),
        P("tp", None),
    )
    out_specs = (P("groups", "hgt", "wid", "tp"), P("groups", "hgt", "wid", "tp"))

    def chosen(*args):
        wid_count = mesh.shape["wid"]
        one_row = mesh.shape["hgt"] == 1 and mesh.shape["tp"] == 2
        even = wid_count % 2 == 0 and args[-1].shape[0] % 2 == 0
        if one_row and even:
            return fused_body(wid_count, *args)
        return body(*args)

    return jax.shard_map(chosen, mesh=mesh, in_specs=in_specs, out_specs=out_specs, check_vma=False)
```

```python
import functools
import math

import jax
import jax.numpy as jnp
from jax import lax
from jax.experimental import pallas as pl
from jax.experimental.pallas import tpu as pltpu
from jax.sharding import PartitionSpec as P

TILE = 4


epsilon = 1e-06
masked = -1e30


def padded(value, sides, width):
    for axis, dim in sides:
        count, length = (lax.axis_size(axis), value.shape[dim])
        up = [(i, (i + 1) % count) for i in range(count - 1)]
        down = [(j, i) for i, j in up]
        last = lax.slice_in_dim(value, length - width, length, axis=dim)
        first = lax.slice_in_dim(value, 0, width, axis=dim)
        before = lax.ppermute(last, axis, up)
        after = lax.ppermute(first, axis, down)
        value = jnp.concatenate([before, value, after], axis=dim)
    return value


def grid_positions(frame_count, row_count, col_count, row_start, col_start):
    full_shape = (frame_count, row_count, col_count)
    frame_ids = jnp.arange(frame_count, dtype=jnp.int32)[:, None, None]
    row_ids = jnp.arange(row_count, dtype=jnp.int32)[None, :, None] + row_start
    col_ids = jnp.arange(col_count, dtype=jnp.int32)[None, None, :] + col_start
    return (
        jnp.broadcast_to(frame_ids, full_shape).reshape(-1),
        jnp.broadcast_to(row_ids, full_shape).reshape(-1),
        jnp.broadcast_to(col_ids, full_shape).reshape(-1),
    )


def window_mask(windows, query_pos, key_pos, height_all, width_all):
    inside = (
        (key_pos[1] >= 0) & (key_pos[1] < height_all) & (key_pos[2] >= 0) & (key_pos[2] < width_all)
    )
    frame_gap = jnp.abs(query_pos[0][:, None] - key_pos[0][None, :])
    row_gap = jnp.abs(query_pos[1][:, None] // TILE - key_pos[1][None, :] // TILE)
    col_gap = jnp.abs(query_pos[2][:, None] // TILE - key_pos[2][None, :] // TILE)
    return (
        (frame_gap[None] <= windows[:, 0, None, None])
        & (row_gap[None] <= windows[:, 1, None, None])
        & (col_gap[None] <= windows[:, 2, None, None])
        & inside[None, None, :]
    )


def attend_part(queries, key_rows, value_rows, allowed):
    factor = 1.0 / math.sqrt(queries.shape[-1])
    scores = (
        jnp.einsum("qhd,khd->hqk", queries, key_rows, preferred_element_type=jnp.float32) * factor
    )
    if allowed is not None:
        scores = jnp.where(allowed, scores, masked)
    row_top = jnp.max(scores, axis=-1)
    powers = jnp.exp(scores - row_top[..., None])
    if allowed is not None:
        powers = jnp.where(allowed, powers, 0.0)
    weights = powers.astype(jnp.bfloat16)
    numerator = jnp.einsum("hqk,khd->hqd", weights, value_rows, preferred_element_type=jnp.float32)
    return (row_top, jnp.sum(powers, axis=-1), numerator)


def merge_parts(first, second):
    row_top = jnp.maximum(first[0], second[0])
    upper = jnp.exp(second[0] - row_top)
    return (row_top, second[1] * upper, second[2] * upper[..., None])


def finish_part(part, frame_count, row_count, col_count):
    heads_out = part[2] / part[1][..., None]
    return jnp.transpose(heads_out, (1, 0, 2)).reshape(frame_count, row_count, col_count, -1)


def sum_squares(field):
    wide = field.astype(jnp.float32)
    return jnp.sum(wide * wide, axis=-1)


def apply_norm(field, squares_all, channel_total, gain):
    inverse = lax.rsqrt(squares_all / channel_total + epsilon)
    return (field.astype(jnp.float32) * inverse[..., None] * gain).astype(jnp.bfloat16)


def flat_heads(field, head_count):
    return field.reshape(-1, head_count, field.shape[-1] // head_count)


def body(
    self_query,
    self_key,
    self_value,
    cross_query,
    text_key,
    text_value,
    image_key,
    image_value,
    query_gain,
    key_gain,
    cross_gain,
    windows,
):
    frame_count, row_count, col_count, channels = self_query.shape
    head_count = windows.shape[0]
    channel_total = channels * lax.axis_size("tp")
    height_all = row_count * lax.axis_size("hgt")
    width_all = col_count * lax.axis_size("wid")
    row_start = lax.axis_index("hgt") * row_count
    col_start = lax.axis_index("wid") * col_count
    squares_all = lax.psum(
        (sum_squares(self_query), sum_squares(self_key), sum_squares(cross_query)), "tp"
    )
    q_normed = apply_norm(self_query, squares_all[0], channel_total, query_gain)
    k_normed = apply_norm(self_key, squares_all[1], channel_total, key_gain)
    x_normed = apply_norm(cross_query, squares_all[2], channel_total, cross_gain)
    queries = flat_heads(q_normed, head_count)
    query_pos = grid_positions(frame_count, row_count, col_count, row_start, col_start)
    stacked = jnp.stack((k_normed, self_value))
    extended = padded(stacked, (("wid", 3), ("hgt", 2)), TILE)
    key_pos = grid_positions(
        frame_count, row_count + 2 * TILE, col_count + 2 * TILE, row_start - TILE, col_start - TILE
    )
    allowed = window_mask(windows, query_pos, key_pos, height_all, width_all)
    self_part = attend_part(
        queries, flat_heads(extended[0], head_count), flat_heads(extended[1], head_count), allowed
    )
    self_out = finish_part(self_part, frame_count, row_count, col_count).astype(jnp.bfloat16)
    crosses = flat_heads(x_normed, head_count)
    query_total = crosses.shape[0]
    start_part = (
        jnp.full((head_count, query_total), masked, jnp.float32),
        jnp.zeros((head_count, query_total), jnp.float32),
        jnp.zeros((head_count, query_total, crosses.shape[-1]), jnp.float32),
    )
    fresh = attend_part(
        crosses,
        flat_heads(lax.all_gather(text_key, "wid", axis=0, tiled=True), head_count),
        flat_heads(lax.all_gather(text_value, "wid", axis=0, tiled=True), head_count),
        None,
    )
    text_part = merge_parts(start_part, fresh)
    image_part = attend_part(
        crosses, flat_heads(image_key, head_count), flat_heads(image_value, head_count), None
    )
    cross_out = (
        finish_part(text_part, frame_count, row_count, col_count)
        + finish_part(image_part, frame_count, row_count, col_count)
    ).astype(jnp.bfloat16)
    return (self_out, cross_out)


MESH = pl.DeviceIdType.MESH
GUESTS = 2


def squares_of(ref, head_count, depth, tokens):
    total = jnp.zeros((tokens, depth), jnp.float32)
    for head in range(head_count):
        wide = head_block(ref, head * depth, depth, tokens)
        total = total + wide * wide
    return jnp.sum(total, axis=-1, keepdims=True)


def head_block(ref, start, depth, tokens):
    block = ref[:, :, :, pl.ds(start, depth)]
    return block.astype(jnp.float32).reshape(tokens, depth)


def dot_nt(left, right):
    return lax.dot_general(
        left, right, (((1,), (1,)), ((), ())), preferred_element_type=jnp.float32
    )


def soft_mix(scores, value_rows, factor):
    row_top = jnp.max(scores, axis=-1, keepdims=True)
    powers = jnp.exp((scores - row_top) * factor)
    total = jnp.sum(powers, axis=-1, keepdims=True)
    mixed = jnp.dot(
        powers.astype(jnp.bfloat16), value_rows, preferred_element_type=jnp.float32
    )
    return mixed * (1.0 / total)


def guest_heads(wid_count, half_heads):
    return GUESTS if wid_count >= 8 and half_heads > GUESTS else 0


def fused(
    wid_count,
    head_count,
    sq_hbm,
    sk_hbm,
    sv_hbm,
    xq_hbm,
    tk_hbm,
    tv_hbm,
    ik_hbm,
    iv_hbm,
    qg_hbm,
    kg_hbm,
    xg_hbm,
    win_ref,
    so_ref,
    co_ref,
    sq_ref,
    sk_ref,
    sv_ref,
    xq_ref,
    ik_ref,
    iv_ref,
    qg_ref,
    kg_ref,
    xg_ref,
    weights,
    totals,
    guest_in,
    guest_out,
    guest_sem,
    passing,
    transit_sem,
    onward_sem,
    text,
    text_out,
    keys,
    values,
    stat,
    stat_in,
    cross,
    cross_send,
    image_part,
    back_send,
    back_in,
    gaps,
    local_sem,
    text_recv,
    up_send,
    down_send,
    side_send,
    halo_send,
    halo_recv,
    stat_send,
    stat_recv,
    cross_sem,
    back_send_sem,
    back_recv_sem,
):
    frames, rows, cols, channels = sq_ref.shape
    tokens = frames * rows * cols
    depth = channels // head_count
    half_heads = head_count // 2
    half = half_heads * depth
    edge = frames * rows * TILE
    col_tiles = cols // TILE
    lines = wid_count // 2
    factor = 1.0 / math.sqrt(depth)
    guests = guest_heads(wid_count, half_heads)
    kept = half - guests * depth

    w = lax.axis_index("wid")
    core = lax.axis_index("tp")
    line = w // 2
    side = w % 2
    mate = line * 2 + (1 - side)
    not_first, not_last = w > 0, w < wid_count - 1
    has_down, has_up = line > 0, line < lines - 1
    is_end = (line == 0) | (line == lines - 1)
    is_host = (line == 1) | (line == lines - 2)
    guest_peer = w + jnp.where((line == 0) | (line == lines - 2), 2, -2)

    def at_wid(target):
        return {"wid": target}

    mine = pl.multiple_of(side * half, depth)
    other = pl.multiple_of((1 - side) * half, depth)
    loads = [
        pltpu.make_async_copy(source, target, local_sem.at[at])
        for at, (source, target) in enumerate(
            (
                (tk_hbm.at[:, pl.ds(mine, half)], text.at[0, w]),
                (tk_hbm.at[:, pl.ds(other, half)], text_out.at[0]),
                (tv_hbm.at[:, pl.ds(mine, half)], text.at[1, w]),
                (tv_hbm.at[:, pl.ds(other, half)], text_out.at[1]),
                (sq_hbm, sq_ref),
                (sk_hbm, sk_ref),
                (xq_hbm, xq_ref),
                (sv_hbm, sv_ref),
                (kg_hbm, kg_ref),
                (xg_hbm, xg_ref),
                (qg_hbm, qg_ref),
                (ik_hbm, ik_ref),
                (iv_hbm, iv_ref),
            )
        )
    ]
    for load in loads:
        load.start()

    barrier = pltpu.get_barrier_semaphore()
    pl.semaphore_signal(barrier, inc=1, device_id={"tp": 1 - core}, device_id_type=MESH)
    for cond, target in (
        (not_first, w - 1),
        (not_last, w + 1),
        (has_down, w - 2),
        (has_up, w + 2),
    ):

        @pl.when(cond)
        def _():
            pl.semaphore_signal(barrier, inc=1, device_id=at_wid(target), device_id_type=MESH)

    expected = 1
    for cond in (not_first, not_last, has_down, has_up):
        expected = expected + jnp.where(cond, 1, 0)
    pl.semaphore_wait(barrier, expected)

    def slot_of(kind, slot, part):
        if part:
            return text.at[kind, slot, :, pl.ds(0, kept)]
        return text.at[kind, slot]

    def relay(kind, slot, up, part):
        return pltpu.make_async_remote_copy(
            src_ref=slot_of(kind, slot, part),
            dst_ref=slot_of(kind, slot, part),
            send_sem=(up_send if up else down_send).at[kind, slot],
            recv_sem=text_recv.at[kind, slot],
            device_id=at_wid(w + 2 if up else w - 2),
            device_id_type=MESH,
        )

    def with_relay(kind, slot, up, cond, act):
        cond = cond & (has_up if up else has_down)
        if guests == 0:
            pl.when(cond)(lambda: act(relay(kind, slot, up, False)))
            return
        near = (line == lines - 2) if up else (line == 1)
        pl.when(cond & near)(lambda: act(relay(kind, slot, up, True)))
        pl.when(cond & jnp.logical_not(near))(lambda: act(relay(kind, slot, up, False)))

    def forward(kind, slot, up):
        with_relay(kind, slot, up, w >= 0, lambda copy: copy.start())

    def take(kind, slot, part=False):
        pltpu.make_async_remote_copy(
            src_ref=slot_of(kind, slot, part),
            dst_ref=slot_of(kind, slot, part),
            send_sem=side_send.at[kind],
            recv_sem=text_recv.at[kind, slot],
            device_id=at_wid(mate),
            device_id_type=MESH,
        ).wait_recv()

    def take_line(kind, slot):
        if guests == 0:
            take(kind, slot)
            return
        pl.when(is_end)(lambda: take(kind, slot, True))
        pl.when(jnp.logical_not(is_end))(lambda: take(kind, slot))

    def relay_step(kind, step, which):
        below, above = (line - step) * 2 + which, (line + step) * 2 + which

        @pl.when(line - step >= 0)
        def _():
            take_line(kind, below)
            forward(kind, below, True)

        @pl.when(line + step < lines)
        def _():
            take_line(kind, above)
            forward(kind, above, False)

    steps = [
        (step, side if turn == 0 else 1 - side) for step in range(1, lines - 1) for turn in range(2)
    ]

    def next_step():
        if steps:
            step, which = steps.pop(0)
            for kind in range(2):
                relay_step(kind, step, which)

    side_copies = []
    for kind in range(2):
        loads[2 * kind].wait()
        forward(kind, w, True)
        forward(kind, w, False)
        loads[2 * kind + 1].wait()
        side_copy = pltpu.make_async_remote_copy(
            src_ref=text_out.at[kind],
            dst_ref=text.at[kind, w],
            send_sem=side_send.at[kind],
            recv_sem=text_recv.at[kind, w],
            device_id=at_wid(mate),
            device_id_type=MESH,
        )
        side_copy.start()
        side_copies.append(side_copy)
    for load in loads[4:11]:
        load.wait()

    lane = lax.broadcasted_iota(jnp.int32, (tokens, depth), 1)
    sums = [squares_of(ref, head_count, depth, tokens) for ref in (sq_ref, sk_ref, xq_ref)]
    stat[...] = jnp.where(lane == 0, sums[0], jnp.where(lane == 1, sums[1], sums[2]))
    stat_copy = pltpu.make_async_remote_copy(
        src_ref=stat,
        dst_ref=stat_in,
        send_sem=stat_send,
        recv_sem=stat_recv,
        device_id={"tp": 1 - core},
        device_id_type=MESH,
    )
    stat_copy.start()

    for kind in range(2):
        take(kind, mate)
        forward(kind, mate, True)
        forward(kind, mate, False)

    place = lax.broadcasted_iota(jnp.int32, (tokens, tokens), 0)
    source = lax.broadcasted_iota(jnp.int32, (tokens, tokens), 1)
    inner = lax.rem(place, edge)
    natural = (
        lax.div(inner, rows * TILE) * (rows * cols)
        + lax.rem(lax.div(inner, TILE), rows) * cols
        + lax.div(place, edge) * TILE
        + lax.rem(inner, TILE)
    )
    to_tiles = jnp.where(natural == source, 1.0, 0.0).astype(jnp.bfloat16)

    def tile_order(block):
        return jnp.dot(to_tiles, block, preferred_element_type=jnp.float32).astype(jnp.bfloat16)

    def halo(ref, at, down):
        return pltpu.make_async_remote_copy(
            src_ref=ref.at[pl.ds(edge if down else tokens, edge)],
            dst_ref=ref.at[pl.ds(edge + tokens if down else 0, edge)],
            send_sem=halo_send.at[at],
            recv_sem=halo_recv.at[at],
            device_id=at_wid(w - 1 if down else w + 1),
            device_id_type=MESH,
        )

    to_line = jnp.where(side == 1, has_up, has_down)
    from_line = jnp.where(side == 1, has_down, has_up)

    def transit(ref, at):
        return pltpu.make_async_remote_copy(
            src_ref=ref.at[pl.ds(pl.multiple_of(jnp.where(side == 1, tokens, edge), 16), edge)],
            dst_ref=passing.at[at // 2],
            send_sem=transit_sem.at[at],
            recv_sem=transit_sem.at[at + 1],
            device_id=at_wid(jnp.where(side == 1, w + 2, w - 2)),
            device_id_type=MESH,
        )

    def onward(ref, at):
        start = pl.multiple_of(jnp.where(side == 1, 0, edge + tokens), 16)
        return pltpu.make_async_remote_copy(
            src_ref=passing.at[at // 2],
            dst_ref=ref.at[pl.ds(start, edge)],
            send_sem=onward_sem.at[at // 2],
            recv_sem=halo_recv.at[jnp.where(side == 1, at + 1, at)],
            device_id=at_wid(mate),
            device_id_type=MESH,
        )

    def pass_on(ref, at):
        @pl.when(from_line)
        def _():
            transit(ref, at).wait_recv()
            onward(ref, at).start()

    def start_halo(ref, at):
        pl.when(to_line)(lambda: transit(ref, at).start())
        pl.when(side == 1)(lambda: halo(ref, at, True).start())
        pl.when(side == 0)(lambda: halo(ref, at + 1, False).start())

    @pl.when(w == 0)
    def _():
        for ref in (keys, values):
            ref[0:edge] = jnp.zeros((edge, channels), jnp.bfloat16)

    @pl.when(w == wid_count - 1)
    def _():
        for ref in (keys, values):
            ref[edge + tokens :] = jnp.zeros((edge, channels), jnp.bfloat16)

    for head in range(head_count):
        block = head_block(sv_ref, head * depth, depth, tokens).astype(jnp.bfloat16)
        values[edge : edge + tokens, head * depth : (head + 1) * depth] = tile_order(block)
    start_halo(values, 2)

    stat_copy.wait()
    whole = stat[...] + stat_in[...]
    inverse = lax.rsqrt(whole / (channels * 2) + epsilon)
    inverse_q, inverse_k, inverse_x = inverse[:, 0:1], inverse[:, 1:2], inverse[:, 2:3]

    def normed(ref, gain_ref, start, inverse_of):
        wide = head_block(ref, start, depth, tokens)
        return (wide * inverse_of * gain_ref[pl.ds(start, depth)][None]).astype(jnp.bfloat16)

    for head in range(head_count):
        block = normed(sk_ref, kg_ref, head * depth, inverse_k)
        keys[edge : edge + tokens, head * depth : (head + 1) * depth] = tile_order(block)
    start_halo(keys, 0)
    next_step()
    pass_on(values, 2)

    for head in range(half_heads):
        at = pl.multiple_of((1 - side) * half + head * depth, depth)
        cross_send[:, head * depth : (head + 1) * depth] = normed(xq_ref, xg_ref, at, inverse_x)
    cross_copy = pltpu.make_async_remote_copy(
        src_ref=cross_send,
        dst_ref=cross.at[pl.ds(tokens, tokens)],
        send_sem=cross_sem.at[0],
        recv_sem=cross_sem.at[1],
        device_id=at_wid(mate),
        device_id_type=MESH,
    )
    cross_copy.start()
    pass_on(keys, 0)

    for head in range(half_heads):
        at = pl.multiple_of(side * half + head * depth, depth)
        cross[0:tokens, head * depth : (head + 1) * depth] = normed(xq_ref, xg_ref, at, inverse_x)

    spread = (tokens, tokens + 2 * edge)
    query = lax.broadcasted_iota(jnp.int32, spread, 0)
    key = lax.broadcasted_iota(jnp.int32, spread, 1)
    key_tile = lax.div(key, edge) - 1
    key_inner = lax.rem(key, edge)
    key_col = key_tile + w * col_tiles
    inside = (key_col >= 0) & (key_col < wid_count * col_tiles)
    frame_gap = jnp.abs(lax.div(query, rows * cols) - lax.div(key_inner, rows * TILE))
    row_gap = jnp.abs(
        lax.div(lax.rem(lax.div(query, cols), rows), TILE)
        - lax.div(lax.rem(lax.div(key_inner, TILE), rows), TILE)
    )
    col_gap = jnp.abs(lax.div(lax.rem(query, cols), TILE) - key_tile)
    gaps[0] = jnp.where(inside, frame_gap, 1 << 30)
    gaps[1] = row_gap
    gaps[2] = col_gap

    def self_head(head):
        at = slice(head * depth, (head + 1) * depth)
        queries = normed(sq_ref, qg_ref, head * depth, inverse_q)
        scores = dot_nt(queries, keys[:, at])
        allowed = (
            (gaps[0] <= win_ref[0, head])
            & (gaps[1] <= win_ref[1, head])
            & (gaps[2] <= win_ref[2, head])
        )
        mixed = soft_mix(jnp.where(allowed, scores, masked), values[:, at], factor)
        so_ref[:, :, :, at] = mixed.reshape(frames, rows, cols, depth).astype(jnp.bfloat16)

    def image_head(head):
        at = slice(head * depth, (head + 1) * depth)
        there = pl.ds(pl.multiple_of(side * half + head * depth, depth), depth)
        scores = dot_nt(cross[:, at], ik_ref[:, there])
        image_part[:, at] = soft_mix(scores, iv_ref[:, there], factor)

    next_step()
    cross_copy.wait_recv()

    def guest_copy(result):
        return pltpu.make_async_remote_copy(
            src_ref=guest_out if result else cross.at[:, pl.ds(kept, guests * depth)],
            dst_ref=guest_in,
            send_sem=guest_sem.at[2 if result else 0],
            recv_sem=guest_sem.at[3 if result else 1],
            device_id=at_wid(guest_peer),
            device_id_type=MESH,
        )

    if guests:
        pl.when(is_end)(lambda: guest_copy(False).start())
    loads[11].wait()
    loads[12].wait()
    for head in range(half_heads):
        image_head(head)
        if head == half_heads // 2 - 1:
            next_step()
    while steps:
        next_step()

    def wait_halo(ref, at):
        @pl.when(not_last)
        def _():
            halo(ref, at, True).wait_recv()

        @pl.when(not_first)
        def _():
            halo(ref, at + 1, False).wait_recv()

    wait_halo(values, 2)
    wait_halo(keys, 0)
    for head in range(head_count):
        self_head(head)

    def last_step(kind):
        if lines > 1:
            for which in range(2):
                relay_step(kind, lines - 1, which)

    rows_all = wid_count * tk_hbm.shape[0]
    def text_weights(queries, at):
        scores = dot_nt(queries, text[0, :, :, at].reshape(rows_all, depth))
        row_top = jnp.max(scores, axis=-1, keepdims=True)
        powers = jnp.exp((scores - row_top) * factor)
        total = jnp.sum(powers, axis=-1, keepdims=True)
        return powers.astype(jnp.bfloat16), 1.0 / total

    def text_mix(shares, at):
        return jnp.dot(
            shares,
            text[1, :, :, at].reshape(rows_all, depth),
            preferred_element_type=jnp.float32,
        )

    def columns(head):
        return slice(head * depth, (head + 1) * depth)

    def weigh(head):
        at = columns(head)
        shares, inverse_total = text_weights(cross[:, at], at)
        totals[:, at] = jnp.broadcast_to(inverse_total, (2 * tokens, depth))
        weights[head] = shares

    def back(head):
        return pltpu.make_async_remote_copy(
            src_ref=back_send.at[head],
            dst_ref=back_in.at[head],
            send_sem=back_send_sem.at[head],
            recv_sem=back_recv_sem.at[head],
            device_id=at_wid(mate),
            device_id_type=MESH,
        )

    def give(head, mixed):
        back_send[head] = mixed[tokens:].astype(jnp.bfloat16)
        back(head).start()
        there = pl.ds(pl.multiple_of(side * half + head * depth, depth), depth)
        own = mixed[:tokens].astype(jnp.float32).reshape(frames, rows, cols, depth)
        co_ref[:, :, :, there] = own.astype(jnp.bfloat16)

    def mix(head):
        at = columns(head)
        give(head, text_mix(weights[head], at) * totals[:, at] + image_part[:, at])

    kept_heads = half_heads - guests
    last_step(0)
    for head in range(kept_heads):
        weigh(head)
    if guests:

        @pl.when(jnp.logical_not(is_end))
        def _():
            for head in range(kept_heads, half_heads):
                weigh(head)

    last_step(1)
    if guests:

        @pl.when(is_host)
        def _():
            guest_copy(False).wait_recv()
            for guest in range(guests):
                at = columns(kept_heads + guest)
                queries = guest_in[:, columns(guest)]
                shares, inverse_total = text_weights(queries, at)
                mixed = text_mix(shares, at) * inverse_total
                first = side * half + (kept_heads + guest) * depth
                there = pl.ds(pl.multiple_of(first, depth), depth)
                scores = dot_nt(queries, ik_ref[:, there])
                mixed = mixed + soft_mix(scores, iv_ref[:, there], factor)
                guest_out[:, columns(guest)] = mixed.astype(jnp.bfloat16)
            guest_copy(True).start()

    for head in range(kept_heads):
        mix(head)
    if guests:

        @pl.when(jnp.logical_not(is_end))
        def _():
            for head in range(kept_heads, half_heads):
                mix(head)

        @pl.when(is_end)
        def _():
            guest_copy(True).wait_recv()
            for guest in range(guests):
                give(kept_heads + guest, guest_in[:, columns(guest)])
            guest_copy(False).wait_send()

        @pl.when(is_host)
        def _():
            guest_copy(True).wait_send()

    for side_copy in side_copies:
        side_copy.wait_send()
    cross_copy.wait_send()
    for at, ref in ((0, keys), (2, values)):

        pl.when(to_line)(lambda: transit(ref, at).wait_send())
        pl.when(from_line)(lambda: onward(ref, at).wait_send())
        pl.when(side == 1)(lambda: halo(ref, at, True).wait_send())
        pl.when(side == 0)(lambda: halo(ref, at + 1, False).wait_send())

    for place_line in range(lines):
        for place_side in range(2):
            slot = place_line * 2 + place_side

            for kind in range(2):
                with_relay(kind, slot, True, place_line <= line, lambda copy: copy.wait_send())
                with_relay(kind, slot, False, place_line >= line, lambda copy: copy.wait_send())

    for head in range(half_heads):
        back(head).wait()
        there = pl.ds(pl.multiple_of((1 - side) * half + head * depth, depth), depth)
        came = back_in[head].astype(jnp.float32).reshape(frames, rows, cols, depth)
        co_ref[:, :, :, there] = came.astype(jnp.bfloat16)


def fused_body(
    wid_count,
    self_query,
    self_key,
    self_value,
    cross_query,
    text_key,
    text_value,
    image_key,
    image_value,
    query_gain,
    key_gain,
    cross_gain,
    windows,
):
    frames, rows, cols, channels = self_query.shape
    tokens = frames * rows * cols
    head_count = windows.shape[0]
    depth = channels // head_count
    half_heads = head_count // 2
    half = half_heads * depth
    edge = frames * rows * TILE
    text_rows = text_key.shape[0]
    guests = guest_heads(wid_count, half_heads)
    bf16, f32 = jnp.bfloat16, jnp.float32
    dma = pltpu.SemaphoreType.DMA
    vmem = pl.BlockSpec(memory_space=pltpu.VMEM)
    return pl.pallas_call(
        functools.partial(fused, wid_count, head_count),
        out_shape=(
            jax.ShapeDtypeStruct(self_query.shape, bf16),
            jax.ShapeDtypeStruct(self_query.shape, bf16),
        ),
        in_specs=[pl.BlockSpec(memory_space=pltpu.HBM)] * 11 + [pl.BlockSpec(memory_space=pltpu.SMEM)],
        out_specs=(vmem, vmem),
        scratch_shapes=[
            *[pltpu.VMEM(self_query.shape, bf16)] * 4,
            *[pltpu.VMEM(image_key.shape, bf16)] * 2,
            *[pltpu.VMEM((channels,), f32)] * 3,
            pltpu.VMEM((half_heads, 2 * tokens, wid_count * text_rows), bf16),
            pltpu.VMEM((2 * tokens, half), f32),
            *[pltpu.VMEM((2 * tokens, max(guests, 1) * depth), bf16)] * 2,
            dma((4,)),
            pltpu.VMEM((2, edge, channels), bf16),
            dma((4,)),
            dma((2,)),
            pltpu.VMEM((2, wid_count, text_rows, half), bf16),
            pltpu.VMEM((2, text_rows, half), bf16),
            pltpu.VMEM((tokens + 2 * edge, channels), bf16),
            pltpu.VMEM((tokens + 2 * edge, channels), bf16),
            pltpu.VMEM((tokens, depth), f32),
            pltpu.VMEM((tokens, depth), f32),
            pltpu.VMEM((2 * tokens, half), bf16),
            pltpu.VMEM((tokens, half), bf16),
            pltpu.VMEM((2 * tokens, half), f32),
            pltpu.VMEM((half_heads, tokens, depth), bf16),
            pltpu.VMEM((half_heads, tokens, depth), bf16),
            pltpu.VMEM((3, tokens, tokens + 2 * edge), jnp.int32),
            dma((13,)),
            dma((2, wid_count)),
            dma((2, wid_count)),
            dma((2, wid_count)),
            dma((2,)),
            dma((4,)),
            dma((4,)),
            dma,
            dma,
            dma((2,)),
            dma((half_heads,)),
            dma((half_heads,)),
        ],
        compiler_params=pltpu.CompilerParams(
            collective_id=0, has_side_effects=True, vmem_limit_bytes=56 * 1024 * 1024
        ),
        name="attention",
    )(
        self_query,
        self_key,
        self_value,
        cross_query,
        text_key,
        text_value,
        image_key,
        image_value,
        query_gain,
        key_gain,
        cross_gain,
        windows.T,
    )


def solution(mesh):
    in_specs = (
        P("groups", "hgt", "wid", "tp"),
        P("groups", "hgt", "wid", "tp"),
        P("groups", "hgt", "wid", "tp"),
        P("groups", "hgt", "wid", "tp"),
        P(("groups", "wid"), "tp"),
        P(("groups", "wid"), "tp"),
        P("groups", "tp"),
        P("groups", "tp"),
        P("tp"),
        P("tp"),
        P("tp"),
        P("tp", None),
    )
    out_specs = (P("groups", "hgt", "wid", "tp"), P("groups", "hgt", "wid", "tp"))

    def chosen(*args):
        wid_count = mesh.shape["wid"]
        one_row = mesh.shape["hgt"] == 1 and mesh.shape["tp"] == 2
        even = wid_count % 2 == 0 and args[-1].shape[0] % 2 == 0
        if one_row and even:
            return fused_body(wid_count, *args)
        return body(*args)

    return jax.shard_map(chosen, mesh=mesh, in_specs=in_specs, out_specs=out_specs, check_vma=False)
```
